128 devices in a mesh: cells: 32 (over y, z, core), edges: 4 (over x).
Axes of the slice: x: 4, y: 4, z: 4, core: 2. Of those that a mesh axis runs over, the one named last changes fastest.
Arguments:
- cells_in: bfloat16 [262144, 768], P(('cells', 'edges')), may hold values from -6 to 6
- w_in: bfloat16 [768, 768], replicated, may hold values from -0.21875 to 0.21875
- w_edge: bfloat16 [768, 768], replicated, may hold values from -0.21875 to 0.21875
- w_out: bfloat16 [768, 768], replicated, may hold values from -0.21875 to 0.21875
- cotangent: bfloat16 [262144, 768], P(('cells', 'edges')), may hold values from -6 to 6
- cell_row: int32 [262144], P(('cells', 'edges')), may hold values from 0 to 255
- send_slot: int32 [2, 262144], P(None, ('cells', 'edges')), may hold values from 0 to 127, as said below
- recv_target: int32 [128, 128], P(('cells', 'edges')), may hold values from 0 to 256, as said below
Outputs:
- layer_out: bfloat16 [262144, 768], P(('cells', 'edges'))
- grad_cells: bfloat16 [262144, 768], P(('cells', 'edges'))
- grad_win: float32 [768, 768], replicated
- grad_wedge: float32 [768, 768], replicated
- grad_wout: float32 [768, 768], replicated
The draws below stay inside these ranges and needn't reach their ends.
Inputs may be any that keep to these rules, and one draw needn't show every extreme that they name: send_slot[k, i] is a slot of the device holding cell i; slot j goes to the device at place j // 32 of that device's group of 4, and every slot that a cell names is live at that owner. recv_target[d, e * 32 + c] is the hyperedge among those device d owns that slot (d % 4) * 32 + c of the device at place e of d's group feeds, or 256 for a slot that carries nothing; live slots of one source to one owner come first, each source has at least one live slot to every owner of its group, and some owner of each group receives 32 live slots from every source of the group. cell_row[i] is the row of cell i among the rows of the device holding it.
All inputs are finite; a program needn't handle non-finite values.
Results may differ from the reference program's by a relative error of at most 0.015.
Values may be sent and summed in bfloat16 or wider, within the bound.
A program may use at most 128 MiB of HBM per device.

```python
import jax
import jax.numpy as jnp
from jax import lax

D = 768
CELL_DEV = 2048
CAP = 32
ROWS_DEV = 256
HE_DEV = 256
NCELL = 262144
N_CELLS = 32
N_EDGES = 4


def routing_plan(key):
    devices = N_CELLS * N_EDGES
    key_live, key_full, key_target, key_owner, key_place = jax.random.split(key, 5)
    live_count = jax.random.randint(key_live, (devices, N_EDGES), 1, CAP + 1)
    full_place = jax.random.randint(key_full, (), 0, N_EDGES)
    owner_index = jnp.arange(N_EDGES)[None, :]
    live_count = jnp.where((owner_index == full_place) | (owner_index == N_EDGES - 1), CAP, live_count)
    targets = jax.random.randint(key_target, (devices, N_EDGES, CAP), 0, HE_DEV)
    ncells = CELL_DEV * devices
    holder = jnp.arange(ncells) // CELL_DEV
    owners = jax.random.randint(key_owner, (2, ncells), 0, N_EDGES)
    picked = jax.random.randint(key_place, (2, ncells), 0, 1 << 20)
    places = picked % live_count[holder[None, :], owners]
    slots = owners * CAP + places
    slots = slots.at[1, ncells - 1].set(N_EDGES * CAP - 1)
    return (live_count, targets, slots.astype(jnp.int32))


def draw_send_slot(key, part):
    return routing_plan(key)[2]


def draw_recv_target(key, part):
    devices = N_CELLS * N_EDGES
    live_count, targets, slots = routing_plan(key)
    places = jnp.arange(CAP)[None, None, :]
    marked = jnp.where(places < live_count[:, :, None], targets, HE_DEV)
    grouped = marked.reshape(N_CELLS, N_EDGES, N_EDGES, CAP)
    return jnp.transpose(grouped, (0, 2, 1, 3)).reshape(devices, N_EDGES * CAP).astype(jnp.int32)


def set_ends(result, own_key, least, top_value):
    spot = [jax.random.randint(jax.random.fold_in(own_key, axis), (), 0, length) for axis, length in enumerate(result.shape)]
    main_axis = result.shape.index(max(result.shape))
    neighbour = spot[:main_axis] + [(spot[main_axis] + 1) % result.shape[main_axis]] + spot[main_axis + 1:]
    return result.at[tuple(spot)].set(least).at[tuple(neighbour)].set(top_value)


def level_of(stream_key, shape, cuts, smallest, high):
    def one(dim, shards_of):
        steps = jax.random.uniform(jax.random.fold_in(jax.random.fold_in(stream_key, 6), dim), (shards_of,), jnp.float32, smallest / len(cuts), high / len(cuts))
        return jnp.repeat(jnp.exp(steps), shape[dim] // shards_of).reshape((-1,) + (1,) * (len(shape) - dim - 1))

    loudness = one(*cuts[0])
    for cut in cuts[1:]:
        loudness = loudness * one(*cut)
    return loudness


def bell_draw(stream_key, dims, scale, most, cuts=(), held_as=jnp.bfloat16):
    array = scale * jax.random.normal(stream_key, dims, jnp.float32)
    if cuts:
        array = array * level_of(stream_key, dims, cuts, -0.22, 0.18)
    return jnp.clip(array, -most, most).astype(held_as)


def setup_inputs(seed: int = 0) -> dict:
    keys = jax.random.split(jax.random.key(seed), 9)
    return {
        "cells_in": bell_draw(keys[0], (NCELL, D), 1.0, 6.0, ((0, 128),)),
        "w_in": bell_draw(keys[1], (D, D), D ** -0.5, 0.21875),
        "w_edge": bell_draw(keys[2], (D, D), D ** -0.5, 0.21875),
        "w_out": bell_draw(keys[3], (D, D), D ** -0.5, 0.21875),
        "cotangent": bell_draw(keys[4], (NCELL, D), 1.0, 6.0, ((0, 128),)),
        "cell_row": set_ends(jax.random.randint(keys[5], (NCELL,), 0, ROWS_DEV), jax.random.fold_in(keys[5], 1), 0, ROWS_DEV - 1).astype(jnp.int32),
        "send_slot": draw_send_slot(jax.random.fold_in(keys[8], 71), 0),
        "recv_target": draw_recv_target(jax.random.fold_in(keys[8], 71), 0),
    }


def contract_rows(left, right):
    return lax.dot_general(left, right, (((0,), (0,)), ((), ())), preferred_element_type=jnp.float32)


def times_transpose(left, right):
    return lax.dot_general(left, right, (((1,), (1,)), ((), ())), preferred_element_type=jnp.float32)


def reference(cells_in, w_in, w_edge, w_out, cotangent, cell_row, send_slot, recv_target):
    devices = N_CELLS * N_EDGES
    ncells = cells_in.shape[0]
    holder = (jnp.arange(ncells, dtype=jnp.int32) // CELL_DEV).astype(jnp.int32)
    group_base = ((holder // N_EDGES) * N_EDGES).astype(jnp.int32)
    local_place = (holder % N_EDGES).astype(jnp.int32)
    row_index = (holder * ROWS_DEV + cell_row).astype(jnp.int32)
    owner = (group_base[None, :] + send_slot // CAP).astype(jnp.int32)
    place = (send_slot % CAP).astype(jnp.int32)
    target = recv_target[owner, local_place[None, :] * CAP + place]
    hyper = (owner * HE_DEV + target).astype(jnp.int32)
    nrows = devices * ROWS_DEV
    nedges = devices * HE_DEV
    preact = jnp.dot(cells_in, w_in, preferred_element_type=jnp.float32)
    message = jax.nn.silu(preact).astype(jnp.bfloat16)
    wide = message.astype(jnp.float32)
    ones = jnp.ones((ncells,), jnp.float32)
    row_sums = jax.ops.segment_sum(wide, row_index, nrows)
    row_counts = jax.ops.segment_sum(ones, row_index, nrows)
    edge_sums = jax.ops.segment_sum(wide, hyper[0], nedges) + jax.ops.segment_sum(wide, hyper[1], nedges)
    edge_counts = jax.ops.segment_sum(ones, hyper[0], nedges) + jax.ops.segment_sum(ones, hyper[1], nedges)
    row_mean = (row_sums / (row_counts + 1.0)[:, None]).astype(jnp.bfloat16)
    edge_mean = (edge_sums / (edge_counts + 1.0)[:, None]).astype(jnp.bfloat16)
    row_out = jnp.dot(row_mean, w_edge, preferred_element_type=jnp.float32).astype(jnp.bfloat16)
    edge_out = jnp.dot(edge_mean, w_edge, preferred_element_type=jnp.float32).astype(jnp.bfloat16)
    mixed = (row_out[row_index].astype(jnp.float32) + edge_out[hyper[0]].astype(jnp.float32)
             + edge_out[hyper[1]].astype(jnp.float32)).astype(jnp.bfloat16)
    layer_out = (cells_in.astype(jnp.float32) + jnp.dot(mixed, w_out, preferred_element_type=jnp.float32)).astype(jnp.bfloat16)
    grad_mixed = times_transpose(cotangent, w_out).astype(jnp.bfloat16)
    grad_wout = contract_rows(mixed, cotangent)
    gwide = grad_mixed.astype(jnp.float32)
    row_grads = jax.ops.segment_sum(gwide, row_index, nrows).astype(jnp.bfloat16)
    edge_grads = (jax.ops.segment_sum(gwide, hyper[0], nedges) + jax.ops.segment_sum(gwide, hyper[1], nedges)).astype(jnp.bfloat16)
    grad_wedge = contract_rows(row_mean, row_grads) + contract_rows(edge_mean, edge_grads)
    grad_rowsum = (times_transpose(row_grads, w_edge) / (row_counts + 1.0)[:, None]).astype(jnp.bfloat16)
    grad_edgesum = (times_transpose(edge_grads, w_edge) / (edge_counts + 1.0)[:, None]).astype(jnp.bfloat16)
    grad_message = (grad_rowsum[row_index].astype(jnp.float32) + grad_edgesum[hyper[0]].astype(jnp.float32)
                    + grad_edgesum[hyper[1]].astype(jnp.float32))
    sigma = jax.nn.sigmoid(preact)
    grad_pre = (grad_message * sigma * (1.0 + preact * (1.0 - sigma))).astype(jnp.bfloat16)
    grad_cells = (cotangent.astype(jnp.float32) + times_transpose(grad_pre, w_in)).astype(jnp.bfloat16)
    grad_win = contract_rows(cells_in, grad_pre)
    return layer_out, grad_cells, grad_win, grad_wedge, grad_wout
```

```python
import jax
import jax.numpy as jnp
from jax import lax
from jax.experimental import pallas as pl
from jax.experimental.pallas import tpu as pltpu
from jax.sharding import PartitionSpec as P

N = 2048
D = 768
R = 256
H = 256
S = 128
CAP = 32
K = R + S
M = 1024
HALF = D // 2
RA = D // 4
RB = RA // 4
WEDGE, WOUT, WIN = 0, 1, 2

f32 = jnp.float32
bf16 = jnp.bfloat16
NT = (((1,), (1,)), ((), ()))
TN = (((0,), (0,)), ((), ()))


def dot(a, b):
    return jnp.dot(a, b, preferred_element_type=f32)


def dot_nt(a, b):
    return lax.dot_general(a, b, NT, preferred_element_type=f32)


def dot_tn(a, b):
    return lax.dot_general(a, b, TN, preferred_element_type=f32)


def aligned(x, m):
    return pl.multiple_of(x, m)


def kernel(
    cells_h, w_in_h, w_edge_h, w_out_h, cot_h, row_ref, slot_ref, tgt_ref,
    lo_h, gc_h, fin_h,
    cells, cot, w_in, w_edge, w_out, dact, msg, gmix, hot_t, hot, ids,
    means, hgrads, hout, gmean, tgt_t, inv,
    out1, out3, got1, got3, reply2, reply4, cat2, cat4,
    send0, recv0, part, send_a, recv_a, part_b, send_b, recv_b, recv_c, fin,
    in_sem, lo_sem, gc_sem, fin_sem,
    x_ss, x_rs, p_ss, p_rs, a_ss, a_rs, b_ss, b_rs, c_ss, c_rs,
    bg_ss, bg_rs, ag_ss, ag_rs, pg_ss, pg_rs,
):
    ci = lax.axis_index("cells")
    x = lax.axis_index("edges")
    core = lax.rem(ci, 2)
    z = lax.rem(lax.div(ci, 2), 4)
    y = lax.div(ci, 8)

    def on_x(k):
        return {"cells": ci, "edges": lax.rem(x + k, 4)}

    def on_y(k):
        return {"cells": (lax.rem(y + k, 4) * 4 + z) * 2 + core, "edges": x}

    def on_z(k):
        return {"cells": (y * 4 + lax.rem(z + k, 4)) * 2 + core, "edges": x}

    twin = {"cells": ci + 1 - 2 * core, "edges": x}
    at = (x, y, z)
    peer = (on_x, on_y, on_z)

    loads = {}

    def load(name, src, dst, i):
        loads[name] = pltpu.make_async_copy(src, dst, in_sem.at[i])
        loads[name].start()

    load("w_in", w_in_h, w_in, 0)
    load("cells0", cells_h.at[pl.ds(0, M)], cells.at[pl.ds(0, M)], 1)
    load("cells1", cells_h.at[pl.ds(M, M)], cells.at[pl.ds(M, M)], 2)
    load("w_out", w_out_h, w_out, 3)
    load("cot0", cot_h.at[pl.ds(0, M)], cot.at[pl.ds(0, M)], 4)
    load("cot1", cot_h.at[pl.ds(M, M)], cot.at[pl.ds(M, M)], 5)
    load("w_edge", w_edge_h, w_edge, 6)

    barrier = pltpu.get_barrier_semaphore()
    for k in (1, 2, 3):
        for where in peer:
            pl.semaphore_signal(
                barrier, inc=1, device_id=where(k), device_id_type=pl.DeviceIdType.MESH
            )
    pl.semaphore_signal(barrier, inc=1, device_id=twin, device_id_type=pl.DeviceIdType.MESH)

    started = []

    def send(src, dst, ss, rs, where):
        copy = pltpu.make_async_remote_copy(
            src_ref=src, dst_ref=dst, send_sem=ss, recv_sem=rs,
            device_id=where, device_id_type=pl.DeviceIdType.MESH,
        )
        copy.start()
        started.append(copy)
        return copy

    ids[...] = jnp.zeros_like(ids)
    ids[0:1, :] = row_ref[...]
    ids[1:3, :] = slot_ref[...]
    tgt_t[...] = (lax.broadcasted_iota(jnp.int32, (H, S), 0) == tgt_ref[...]).astype(bf16)

    def ones_where(mask):
        return jnp.where(mask, 1.0, 0.0)

    for i in range(N // M):
        rows = pl.ds(i * M, M)
        if i == 0:
            loads["w_in"].wait()
        loads["cells%d" % i].wait()
        pre = dot(cells[rows, :], w_in[...])
        sig = 0.5 * jnp.tanh(0.5 * pre) + 0.5
        m = pre * sig
        msg[rows, :] = m.astype(bf16)
        dact[rows, :] = (sig + m * (1.0 - sig)).astype(bf16)
        some = ids[:, rows]
        hot_t[0:R, rows] = ones_where(
            lax.broadcasted_iota(jnp.int32, (R, M), 0) == some[0:1, :]
        ).astype(bf16)
        slot_i = lax.broadcasted_iota(jnp.int32, (S, M), 0)
        hot_t[R:K, rows] = (
            ones_where(slot_i == some[1:2, :]) + ones_where(slot_i == some[2:3, :])
        ).astype(bf16)
        col = some.T
        hot[rows, 0:R] = ones_where(
            lax.broadcasted_iota(jnp.int32, (M, R), 1) == col[:, 0:1]
        ).astype(bf16)
        slot_j = lax.broadcasted_iota(jnp.int32, (M, S), 1)
        hot[rows, R:K] = (
            ones_where(slot_j == col[:, 1:2]) + ones_where(slot_j == col[:, 2:3])
        ).astype(bf16)

    ones = jnp.ones((N, S), bf16)
    out1[:, 0:D] = dot(hot_t[R:K, :], msg[...]).astype(bf16)
    count = dot(hot_t[R:K, :], ones)
    high = jnp.floor(count * (1.0 / 128.0)) * 128.0
    lane = lax.broadcasted_iota(jnp.int32, (S, S), 1)
    out1[:, D:] = jnp.where(lane < S // 2, high, count - high).astype(bf16)

    pl.semaphore_wait(barrier, 10)

    def exchange(kind, src, dst, base):
        mine = pl.ds(aligned(base + x * CAP, CAP), CAP)
        copies = []
        for k in (1, 2, 3):
            theirs = pl.ds(aligned(lax.rem(x + k, 4) * CAP, CAP), CAP)
            copies.append(
                send(src.at[theirs], dst.at[mine], x_ss.at[kind, k - 1], x_rs.at[kind, k - 1], on_x(k))
            )
        dst[mine, :] = src[pl.ds(aligned(x * CAP, CAP), CAP), :]
        return copies

    x1 = exchange(0, out1, got1, 0)

    loads["w_out"].wait()
    for i in range(N // M):
        rows = pl.ds(i * M, M)
        loads["cot%d" % i].wait()
        gmix[rows, :] = dot_nt(cot[rows, :], w_out[...]).astype(bf16)
    out3[...] = dot(hot_t[R:K, :], gmix[...]).astype(bf16)
    x3 = exchange(1, out3, got3, 0)

    loads["w_edge"].wait()
    inv[0:R, :] = 1.0 / (dot(hot_t[0:R, :], ones) + 1.0)
    means[0:R, :] = (dot(hot_t[0:R, :], msg[...]) * inv[0:R, 0:1]).astype(bf16)
    for copy in x1:
        copy.wait_recv()
    counted = dot(tgt_t[...], got1[:, D:])
    inv[R:, :] = jnp.broadcast_to(
        1.0 / (counted[:, 0:1] + counted[:, S // 2 : S // 2 + 1] + 1.0), (H, S)
    )
    means[R:, :] = (dot(tgt_t[...], got1[:, 0:D]) * inv[R:, 0:1]).astype(bf16)
    hout[...] = dot(means[R:, :], w_edge[...]).astype(bf16)
    reply2[...] = dot_tn(tgt_t[...], hout[...]).astype(bf16)
    x2 = exchange(2, reply2, cat2, R)
    cat2[0:R, :] = dot(means[0:R, :], w_edge[...]).astype(bf16)
    hgrads[0:R, :] = dot(hot_t[0:R, :], gmix[...]).astype(bf16)
    for copy in x3:
        copy.wait_recv()
    hgrads[R:, :] = dot(tgt_t[...], got3[...]).astype(bf16)
    gmean[...] = (dot_nt(hgrads[R:, :], w_edge[...]) * inv[R:, 0:1]).astype(bf16)
    reply4[...] = dot_tn(tgt_t[...], gmean[...]).astype(bf16)
    x4 = exchange(3, reply4, cat4, R)
    cat4[0:R, :] = (dot_nt(hgrads[0:R, :], w_edge[...]) * inv[0:R, 0:1]).astype(bf16)

    near = pl.ds(aligned(core * HALF, 128), HALF)
    far = pl.ds(aligned((1 - core) * HALF, 128), HALF)
    axes = ((0, 1, 2), (1, 2, 0), (2, 0, 1))
    held = {}

    def gradient(g, left, right):
        send0[g] = dot_tn(left[...], right[:, far]).astype(bf16)
        held[g, "p"] = send(send0.at[g], recv0.at[g], p_ss.at[g], p_rs.at[g], twin)
        part[g] = dot_tn(left[...], right[:, near])

    def step_a(g):
        held[g, "p"].wait_recv()
        total = part[g] + recv0[g].astype(f32)
        part[g] = total
        send_a[g] = total.astype(bf16)
        for t in range(3):
            ax = axes[t][0]
            for k in (1, 2, 3):
                theirs = pl.ds(aligned(lax.rem(at[ax] + k, 4) * RA, RA), RA)
                held[g, "a", t, k] = send(
                    send_a.at[g, theirs, pl.ds(t * 128, 128)], recv_a.at[g, k - 1, t],
                    a_ss.at[g, t, k - 1], a_rs.at[g, t, k - 1], peer[ax](k),
                )

    def step_b(g):
        for t in range(3):
            ax = axes[t][1]
            mine = pl.ds(aligned(at[axes[t][0]] * RA, RA), RA)
            total = part[g, mine, t * 128 : (t + 1) * 128]
            for k in (1, 2, 3):
                held[g, "a", t, k].wait_recv()
                total = total + recv_a[g, k - 1, t].astype(f32)
            part_b[g, t] = total
            send_b[g, t] = total.astype(bf16)
            for k in (1, 2, 3):
                theirs = pl.ds(aligned(lax.rem(at[ax] + k, 4) * RB, RB), RB)
                held[g, "b", t, k] = send(
                    send_b.at[g, t, theirs], recv_b.at[g, k - 1, t],
                    b_ss.at[g, t, k - 1], b_rs.at[g, t, k - 1], peer[ax](k),
                )

    def step_c(g):
        for t in range(3):
            ax = axes[t][2]
            mine = pl.ds(aligned(at[axes[t][1]] * RB, RB), RB)
            total = part_b[g, t, mine, :]
            for k in (1, 2, 3):
                held[g, "b", t, k].wait_recv()
                total = total + recv_b[g, k - 1, t].astype(f32)
            recv_c[g, t, pl.ds(at[ax], 1)] = total.astype(bf16)[None]
            for k in (1, 2, 3):
                held[g, "c", t, k] = send(
                    recv_c.at[g, t, at[ax]], recv_c.at[g, t, at[ax]],
                    c_ss.at[g, t, k - 1], c_rs.at[g, t, k - 1], peer[ax](k),
                )

    def column(t):
        return pl.ds(aligned(core * HALF + t * 128, 128), 128)

    def gather_b(g):
        for t in range(3):
            ax = axes[t][1]
            for k in (1, 2, 3):
                held[g, "c", t, k].wait_recv()
            total = recv_c[g, t, 0].astype(f32)
            for k in (1, 2, 3):
                total = total + recv_c[g, t, k].astype(f32)
            place = pl.ds(aligned(at[axes[t][0]] * RA + at[ax] * RB, RB), RB)
            fin[g, place, column(t)] = total.astype(bf16)
            block = fin.at[g, place, column(t)]
            for k in (1, 2, 3):
                held[g, "bg", t, k] = send(
                    block, block, bg_ss.at[g, t, k - 1], bg_rs.at[g, t, k - 1], peer[ax](k)
                )

    def gather_a(g):
        for t in range(3):
            ax = axes[t][0]
            for k in (1, 2, 3):
                held[g, "bg", t, k].wait_recv()
            block = fin.at[g, pl.ds(aligned(at[ax] * RA, RA), RA), column(t)]
            for k in (1, 2, 3):
                held[g, "ag", t, k] = send(
                    block, block, ag_ss.at[g, t, k - 1], ag_rs.at[g, t, k - 1], peer[ax](k)
                )

    def gather_p(g):
        for t in range(3):
            for k in (1, 2, 3):
                held[g, "ag", t, k].wait_recv()
            block = fin.at[g, :, column(t)]
            held[g, "pg", t] = send(block, block, pg_ss.at[g, t], pg_rs.at[g, t], twin)

    def finish(g):
        for t in range(3):
            held[g, "pg", t].wait_recv()
        done = pltpu.make_async_copy(fin.at[g], fin_h.at[g], fin_sem.at[g])
        done.start()
        return done

    gradient(WEDGE, means, hgrads)

    mixed = msg
    for copy in x2:
        copy.wait_recv()
    for i in range(N // M):
        rows = pl.ds(i * M, M)
        mixed[rows, :] = dot(hot[rows, :], cat2[...]).astype(bf16)
    step_a(WEDGE)
    gradient(WOUT, mixed, cot)
    step_b(WEDGE)
    gpre = gmix
    for copy in x4:
        copy.wait_recv()
    for i in range(N // M):
        rows = pl.ds(i * M, M)
        gpre[rows, :] = (dot(hot[rows, :], cat4[...]) * dact[rows, :].astype(f32)).astype(bf16)
    step_a(WOUT)
    step_c(WEDGE)
    gradient(WIN, cells, gpre)
    gather_b(WEDGE)
    step_a(WIN)
    step_b(WOUT)

    stores = []

    def layer_out(i):
        rows = pl.ds(i * M, M)
        mixed[rows, :] = (cells[rows, :].astype(f32) + dot(mixed[rows, :], w_out[...])).astype(bf16)
        done = pltpu.make_async_copy(mixed.at[rows], lo_h.at[rows], lo_sem.at[i])
        done.start()
        stores.append(done)

    def grad_cells(i):
        rows = pl.ds(i * M, M)
        gpre[rows, :] = (cot[rows, :].astype(f32) + dot_nt(gpre[rows, :], w_in[...])).astype(bf16)
        done = pltpu.make_async_copy(gpre.at[rows], gc_h.at[rows], gc_sem.at[i])
        done.start()
        stores.append(done)

    layer_out(0)
    gather_a(WEDGE)
    step_c(WOUT)
    step_b(WIN)
    layer_out(1)
    gather_b(WOUT)
    step_c(WIN)
    gather_p(WEDGE)
    grad_cells(0)
    gather_a(WOUT)
    gather_b(WIN)
    stores.append(finish(WEDGE))
    grad_cells(1)
    gather_a(WIN)
    gather_p(WOUT)
    stores.append(finish(WOUT))
    gather_p(WIN)
    stores.append(finish(WIN))
    for done in stores:
        done.wait()
    for copy in started:
        copy.wait_send()


def per_device(cells_in, w_in, w_edge, w_out, cotangent, cell_row, send_slot, recv_target):
    any_spec = pl.BlockSpec(memory_space=pl.ANY)
    vmem = pl.BlockSpec(memory_space=pltpu.VMEM)
    dma = pltpu.SemaphoreType.DMA
    scratch = [
        pltpu.VMEM((N, D), bf16),
        pltpu.VMEM((N, D), bf16),
        pltpu.VMEM((D, D), bf16),
        pltpu.VMEM((D, D), bf16),
        pltpu.VMEM((D, D), bf16),
        pltpu.VMEM((N, D), bf16),
        pltpu.VMEM((N, D), bf16),
        pltpu.VMEM((N, D), bf16),
        pltpu.VMEM((K, N), bf16),
        pltpu.VMEM((N, K), bf16),
        pltpu.VMEM((8, N), jnp.int32),
        pltpu.VMEM((R + H, D), bf16),
        pltpu.VMEM((R + H, D), bf16),
        pltpu.VMEM((H, D), bf16),
        pltpu.VMEM((H, D), bf16),
        pltpu.VMEM((H, S), bf16),
        pltpu.VMEM((R + H, S), f32),
        pltpu.VMEM((S, D + S), bf16),
        pltpu.VMEM((S, D), bf16),
        pltpu.VMEM((S, D + S), bf16),
        pltpu.VMEM((S, D), bf16),
        pltpu.VMEM((S, D), bf16),
        pltpu.VMEM((S, D), bf16),
        pltpu.VMEM((K, D), bf16),
        pltpu.VMEM((K, D), bf16),
        pltpu.VMEM((3, D, HALF), bf16),
        pltpu.VMEM((3, D, HALF), bf16),
        pltpu.VMEM((3, D, HALF), f32),
        pltpu.VMEM((3, D, HALF), bf16),
        pltpu.VMEM((3, 3, 3, RA, 128), bf16),
        pltpu.VMEM((3, 3, RA, 128), f32),
        pltpu.VMEM((3, 3, RA, 128), bf16),
        pltpu.VMEM((3, 3, 3, RB, 128), bf16),
        pltpu.VMEM((3, 3, 4, RB, 128), bf16),
        pltpu.VMEM((3, D, D), bf16),
        dma((7,)),
        dma((2,)),
        dma((2,)),
        dma((3,)),
        dma((4, 3)),
        dma((4, 3)),
        dma((3,)),
        dma((3,)),
        dma((3, 3, 3)),
        dma((3, 3, 3)),
        dma((3, 3, 3)),
        dma((3, 3, 3)),
        dma((3, 3, 3)),
        dma((3, 3, 3)),
        dma((3, 3, 3)),
        dma((3, 3, 3)),
        dma((3, 3, 3)),
        dma((3, 3, 3)),
        dma((3, 3)),
        dma((3, 3)),
    ]
    layer_out, grad_cells, fin = pl.pallas_call(
        kernel,
        out_shape=(
            jax.ShapeDtypeStruct((N, D), bf16),
            jax.ShapeDtypeStruct((N, D), bf16),
            jax.ShapeDtypeStruct((3, D, D), bf16),
        ),
        in_specs=[any_spec] * 5 + [vmem] * 3,
        out_specs=(any_spec, any_spec, any_spec),
        scratch_shapes=scratch,
        compiler_params=pltpu.CompilerParams(
            collective_id=0, has_side_effects=True, vmem_limit_bytes=56 * 2**20
        ),
        name="layer",
    )(
        cells_in, w_in, w_edge, w_out, cotangent,
        cell_row.reshape(1, N), send_slot, recv_target,
    )
    wide = fin.astype(f32)
    return layer_out, grad_cells, wide[WIN], wide[WEDGE], wide[WOUT]


def solution(mesh):
    placed = (
        P(("cells", "edges"), None),
        P(),
        P(),
        P(),
        P(("cells", "edges"), None),
        P(("cells", "edges")),
        P(None, ("cells", "edges")),
        P(("cells", "edges"), None),
    )
    return jax.shard_map(
        per_device,
        mesh=mesh,
        in_specs=placed,
        out_specs=(P(("cells", "edges"), None), P(("cells", "edges"), None), P(), P(), P()),
        check_vma=False,
    )
```

```python
import jax
import jax.numpy as jnp
from jax import lax
from jax.experimental import pallas as pl
from jax.experimental.pallas import tpu as pltpu
from jax.sharding import PartitionSpec as P

N = 2048
D = 768
R = 256
H = 256
S = 128
CAP = 32
K = R + S
M = 1024
HALF = D // 2
WEDGE, WOUT, WIN = 0, 1, 2
BOTH = (0, 2)
LAST = (2, 1)

f32 = jnp.float32
bf16 = jnp.bfloat16
NT = (((1,), (1,)), ((), ()))
TN = (((0,), (0,)), ((), ()))


def dot(a, b):
    return jnp.dot(a, b, preferred_element_type=f32)


def dot_nt(a, b):
    return lax.dot_general(a, b, NT, preferred_element_type=f32)


def dot_tn(a, b):
    return lax.dot_general(a, b, TN, preferred_element_type=f32)


def aligned(x, m):
    return pl.multiple_of(x, m)


def kernel(
    cells_h, w_in_h, w_edge_h, w_out_h, cot_h, row_h, slot_h, tgt_h,
    mixed, gpre, win_ref, wedge_ref, wout_ref,
    row_ref, slot_ref, tgt_ref, cells, cot, w_in, w_edge, w_out, dact, hot_t, hot, ids,
    means, hgrads, hout, gmean, tgt_t, inv,
    out1, out3, got1, got3, reply2, reply4, cat2, cat4,
    send0, recv0, part, send_a, recv_a, part_b, send_b, recv_b, recv_c, fin,
    in_sem,
    x_ss, x_rs, p_ss, p_rs, a_ss, a_rs, b_ss, b_rs, c_ss, c_rs,
    bg_ss, bg_rs, ag_ss, ag_rs, pg_ss, pg_rs,
):
    ci = lax.axis_index("cells")
    x = lax.axis_index("edges")
    core = lax.rem(ci, 2)
    z = lax.rem(lax.div(ci, 2), 4)
    y = lax.div(ci, 8)

    def on_x(k):
        return {"cells": ci, "edges": lax.rem(x + k, 4)}

    def on_y(k):
        return {"cells": (lax.rem(y + k, 4) * 4 + z) * 2 + core, "edges": x}

    def on_z(k):
        return {"cells": (y * 4 + lax.rem(z + k, 4)) * 2 + core, "edges": x}

    twin = {"cells": ci + 1 - 2 * core, "edges": x}
    at = (x, y, z)
    peer = (on_x, on_y, on_z)

    msg, gmix = mixed, gpre

    loads = {}

    def arrive(name):
        loads.pop(name).wait()

    def load(name, src, dst, i):
        loads[name] = pltpu.make_async_copy(src, dst, in_sem.at[i])
        loads[name].start()

    for i, (name, src, dst) in enumerate(
        (
            ("rows", row_h, row_ref),
            ("slots", slot_h, slot_ref),
            ("targets", tgt_h, tgt_ref),
            ("w_in", w_in_h, w_in),
            ("cells0", cells_h.at[pl.ds(0, M)], cells.at[pl.ds(0, M)]),
            ("cells1", cells_h.at[pl.ds(M, M)], cells.at[pl.ds(M, M)]),
            ("w_out", w_out_h, w_out),
            ("cot0", cot_h.at[pl.ds(0, M)], cot.at[pl.ds(0, M)]),
            ("cot1", cot_h.at[pl.ds(M, M)], cot.at[pl.ds(M, M)]),
            ("w_edge", w_edge_h, w_edge),
        )
    ):
        load(name, src, dst, i)

    barrier = pltpu.get_barrier_semaphore()
    for k in (1, 2, 3):
        for where in peer:
            pl.semaphore_signal(
                barrier, inc=1, device_id=where(k), device_id_type=pl.DeviceIdType.MESH
            )
    pl.semaphore_signal(barrier, inc=1, device_id=twin, device_id_type=pl.DeviceIdType.MESH)

    sent = []

    def send(src, dst, ss, rs, where):
        pltpu.make_async_remote_copy(
            src_ref=src, dst_ref=dst, send_sem=ss, recv_sem=rs,
            device_id=where, device_id_type=pl.DeviceIdType.MESH,
        ).start()

    def take(ref, sem):
        pltpu.make_async_copy(ref, ref, sem).wait()

    for name in ("rows", "slots", "targets"):
        arrive(name)
    ids[...] = jnp.zeros_like(ids)
    ids[0:1, :] = row_ref[...]
    ids[1:3, :] = slot_ref[...]
    tgt_t[...] = (lax.broadcasted_iota(jnp.int32, (H, S), 0) == tgt_ref[...]).astype(bf16)

    def ones_where(mask):
        return jnp.where(mask, 1.0, 0.0)

    def incidences(i):
        rows = pl.ds(i * M, M)
        some = ids[:, rows]
        hot_t[0:R, rows] = ones_where(
            lax.broadcasted_iota(jnp.int32, (R, M), 0) == some[0:1, :]
        ).astype(bf16)
        slot_i = lax.broadcasted_iota(jnp.int32, (S, M), 0)
        hot_t[R:K, rows] = (
            ones_where(slot_i == some[1:2, :]) + ones_where(slot_i == some[2:3, :])
        ).astype(bf16)
        col = some.T
        hot[rows, 0:R] = ones_where(
            lax.broadcasted_iota(jnp.int32, (M, R), 1) == col[:, 0:1]
        ).astype(bf16)
        slot_j = lax.broadcasted_iota(jnp.int32, (M, S), 1)
        hot[rows, R:K] = (
            ones_where(slot_j == col[:, 1:2]) + ones_where(slot_j == col[:, 2:3])
        ).astype(bf16)

    incidences(0)
    arrive("w_in")
    for i in range(N // M):
        rows = pl.ds(i * M, M)
        arrive("cells%d" % i)
        pre = dot(cells[rows, :], w_in[...])
        sig = 0.5 * jnp.tanh(0.5 * pre) + 0.5
        m = pre * sig
        msg[rows, :] = m.astype(bf16)
        dact[rows, :] = (sig + m * (1.0 - sig)).astype(bf16)
        if i == 0:
            incidences(1)

    ones = jnp.ones((N, S), bf16)
    out1[:, 0:D] = dot(hot_t[R:K, :], msg[...]).astype(bf16)
    count = dot(hot_t[R:K, :], ones)
    high = jnp.floor(count * (1.0 / 128.0)) * 128.0
    lane = lax.broadcasted_iota(jnp.int32, (S, S), 1)
    out1[:, D:] = jnp.where(lane < S // 2, high, count - high).astype(bf16)

    pl.semaphore_wait(barrier, 10)

    def exchange(kind, src, dst, base):
        mine = pl.ds(aligned(base + x * CAP, CAP), CAP)
        for k in (2, 1, 3):
            theirs = pl.ds(aligned(lax.rem(x + k, 4) * CAP, CAP), CAP)
            send(src.at[theirs], dst.at[mine], x_ss.at[kind], x_rs.at[kind], on_x(k))
        sent.append((src.at[pl.ds(0, 3 * CAP)], x_ss.at[kind]))
        dst[mine, :] = src[pl.ds(aligned(x * CAP, CAP), CAP), :]

    def arrived(kind, dst):
        take(dst.at[pl.ds(0, 3 * CAP)], x_rs.at[kind])

    exchange(0, out1, got1, 0)

    arrive("w_out")
    for i in range(N // M):
        rows = pl.ds(i * M, M)
        arrive("cot%d" % i)
        gmix[rows, :] = dot_nt(cot[rows, :], w_out[...]).astype(bf16)
    out3[...] = dot(hot_t[R:K, :], gmix[...]).astype(bf16)
    exchange(1, out3, got3, 0)

    arrive("w_edge")
    inv[0:R, :] = 1.0 / (dot(hot_t[0:R, :], ones) + 1.0)
    means[0:R, :] = (dot(hot_t[0:R, :], msg[...]) * inv[0:R, 0:1]).astype(bf16)
    arrived(0, got1)
    counted = dot(tgt_t[...], got1[:, D:])
    inv[R:, :] = jnp.broadcast_to(
        1.0 / (counted[:, 0:1] + counted[:, S // 2 : S // 2 + 1] + 1.0), (H, S)
    )
    means[R:, :] = (dot(tgt_t[...], got1[:, 0:D]) * inv[R:, 0:1]).astype(bf16)
    hout[...] = dot(means[R:, :], w_edge[...]).astype(bf16)
    reply2[...] = dot_tn(tgt_t[...], hout[...]).astype(bf16)
    exchange(2, reply2, cat2, R)
    cat2[0:R, :] = dot(means[0:R, :], w_edge[...]).astype(bf16)
    hgrads[0:R, :] = dot(hot_t[0:R, :], gmix[...]).astype(bf16)
    arrived(1, got3)
    hgrads[R:, :] = dot(tgt_t[...], got3[...]).astype(bf16)
    gmean[...] = (dot_nt(hgrads[R:, :], w_edge[...]) * inv[R:, 0:1]).astype(bf16)
    reply4[...] = dot_tn(tgt_t[...], gmean[...]).astype(bf16)
    exchange(3, reply4, cat4, R)
    cat4[0:R, :] = (dot_nt(hgrads[0:R, :], w_edge[...]) * inv[0:R, 0:1]).astype(bf16)

    near = pl.ds(aligned(core * HALF, 128), HALF)
    far = pl.ds(aligned((1 - core) * HALF, 128), HALF)
    axes = ((0, 1, 2), (1, 2, 0), (2, 0, 1))

    def piece_a(base, t, a):
        return (
            pl.ds(aligned(base + t * 128 + lax.div(a, 2) * 64, 64), 64),
            pl.ds(aligned(lax.rem(a, 2) * HALF, 128), HALF),
        )

    def piece_b(base, t, a, b):
        return (
            pl.ds(aligned(base + t * 128 + lax.div(a, 2) * 64 + b * 16, 16), 16),
            pl.ds(aligned(lax.rem(a, 2) * HALF, 128), HALF),
        )

    def around(ax, k):
        return lax.rem(at[ax] + k, 4)

    def some(span):
        return pl.ds(span[0], span[1])

    def gradient(g, left, right):
        send0[g] = dot_tn(left[:, far], right[...]).astype(bf16)
        send(send0.at[g], recv0.at[g], p_ss.at[g], p_rs.at[g], twin)
        sent.append((send0.at[g], p_ss.at[g]))
        part[g] = dot_tn(left[:, near], right[...])

    def step_a(span):
        gs, q = some(span), span[0]
        for g in range(span[0], span[0] + span[1]):
            take(recv0.at[g], p_rs.at[g])
            send_a[g] = (part[g] + recv0[g].astype(f32)).astype(bf16)
        for k in (2, 1, 3):
            for t in range(3):
                ax = axes[t][0]
                r, c = piece_a(0, t, around(ax, k))
                send(send_a.at[gs, r, c], recv_a.at[k - 1, t, gs], a_ss.at[q], a_rs.at[q], peer[ax](k))
        sent.append((recv_a.at[:, :, gs], a_ss.at[q]))

    def step_b(span):
        gs, q = some(span), span[0]
        take(recv_a.at[:, :, gs], a_rs.at[q])
        for t in range(3):
            ax = axes[t][1]
            r, c = piece_a(0, t, at[axes[t][0]])
            total = part[gs, r, c] + recv0[gs, r, c].astype(f32)
            for k in range(3):
                total = total + recv_a[k, t, gs].astype(f32)
            part_b[t, gs] = total
            send_b[t, gs] = total.astype(bf16)
            for k in (2, 1, 3):
                theirs = pl.ds(aligned(around(ax, k) * 16, 16), 16)
                send(send_b.at[t, gs, theirs], recv_b.at[k - 1, t, gs], b_ss.at[q], b_rs.at[q], peer[ax](k))
        sent.append((recv_b.at[:, :, gs], b_ss.at[q]))

    def step_c(span):
        gs, q = some(span), span[0]
        take(recv_b.at[:, :, gs], b_rs.at[q])
        for t in range(3):
            ax = axes[t][2]
            mine = pl.ds(aligned(at[axes[t][1]] * 16, 16), 16)
            total = part_b[t, gs, mine, :]
            for k in range(3):
                total = total + recv_b[k, t, gs].astype(f32)
            recv_c[pl.ds(at[ax], 1), t, gs] = total.astype(bf16)[None]
            block = recv_c.at[at[ax], t, gs]
            for k in (2, 1, 3):
                send(block, block, c_ss.at[q], c_rs.at[q], peer[ax](k))
        sent.append((recv_b.at[:, :, gs], c_ss.at[q]))

    def gather_b(span):
        gs, q = some(span), span[0]
        take(recv_b.at[:, :, gs], c_rs.at[q])
        for t in range(3):
            ax = axes[t][1]
            total = recv_c[0, t, gs].astype(f32)
            for k in (1, 2, 3):
                total = total + recv_c[k, t, gs].astype(f32)
            r, c = piece_b(core * HALF, t, at[axes[t][0]], at[ax])
            fin[gs, r, c] = total.astype(bf16)
            block = fin.at[gs, r, c]
            for k in (2, 1, 3):
                send(block, block, bg_ss.at[q], bg_rs.at[q], peer[ax](k))
        sent.append((recv_b.at[:, :, gs], bg_ss.at[q]))

    def gather_a(span):
        gs, q = some(span), span[0]
        take(recv_b.at[:, :, gs], bg_rs.at[q])
        for t in range(3):
            ax = axes[t][0]
            r, c = piece_a(core * HALF, t, at[ax])
            block = fin.at[gs, r, c]
            for k in (2, 1, 3):
                send(block, block, ag_ss.at[q], ag_rs.at[q], peer[ax](k))
        sent.append((recv_a.at[:, :, gs], ag_ss.at[q]))

    def gather_p(span):
        gs, q = some(span), span[0]
        take(recv_a.at[:, :, gs], ag_rs.at[q])
        block = fin.at[gs, near]
        send(block, block, pg_ss.at[q], pg_rs.at[q], twin)
        sent.append((block, pg_ss.at[q]))

    def all_sent():
        for ref, sem in sent:
            take(ref, sem)
        sent.clear()

    def finish(span, *outs):
        for g, out in enumerate(outs, span[0]):
            out[near, :] = fin[g, near, :].astype(f32)
        take(fin.at[some(span), far], pg_rs.at[span[0]])
        for g, out in enumerate(outs, span[0]):
            out[far, :] = fin[g, far, :].astype(f32)

    gradient(WEDGE, means, hgrads)
    arrived(2, cat2)
    for i in range(N // M):
        rows = pl.ds(i * M, M)
        mixed[rows, :] = dot(hot[rows, :], cat2[...]).astype(bf16)
    gradient(WOUT, mixed, cot)
    arrived(3, cat4)
    for i in range(N // M):
        rows = pl.ds(i * M, M)
        gpre[rows, :] = (dot(hot[rows, :], cat4[...]) * dact[rows, :].astype(f32)).astype(bf16)
    step_a(BOTH)
    gradient(WIN, cells, gpre)
    step_a(LAST)

    def layer_out(i):
        rows = pl.ds(i * M, M)
        mixed[rows, :] = (cells[rows, :].astype(f32) + dot(mixed[rows, :], w_out[...])).astype(bf16)

    def grad_cells(i):
        rows = pl.ds(i * M, M)
        gpre[rows, :] = (cot[rows, :].astype(f32) + dot_nt(gpre[rows, :], w_in[...])).astype(bf16)

    layer_out(0)
    step_b(BOTH)
    layer_out(1)
    step_b(LAST)
    step_c(BOTH)
    grad_cells(0)
    step_c(LAST)
    gather_b(BOTH)
    grad_cells(1)
    gather_b(LAST)
    gather_a(BOTH)
    gather_a(LAST)
    all_sent()
    gather_p(BOTH)
    gather_p(LAST)
    finish(BOTH, wedge_ref, wout_ref)
    finish(LAST, win_ref)
    all_sent()


def write(*refs):
    n = len(refs) // 2
    copies = [
        pltpu.make_async_copy(refs[i], refs[n + i], refs[2 * n].at[i]) for i in range(n)
    ]
    for copy in copies:
        copy.start()
    for copy in copies:
        copy.wait()


def per_device(cells_in, w_in, w_edge, w_out, cotangent, cell_row, send_slot, recv_target):
    any_spec = pl.BlockSpec(memory_space=pl.ANY)
    vmem = pl.BlockSpec(memory_space=pltpu.VMEM)
    dma = pltpu.SemaphoreType.DMA
    scratch = [
        pltpu.VMEM((1, N), jnp.int32),
        pltpu.VMEM((2, N), jnp.int32),
        pltpu.VMEM((1, S), jnp.int32),
        pltpu.VMEM((N, D), bf16),
        pltpu.VMEM((N, D), bf16),
        pltpu.VMEM((D, D), bf16),
        pltpu.VMEM((D, D), bf16),
        pltpu.VMEM((D, D), bf16),
        pltpu.VMEM((N, D), bf16),
        pltpu.VMEM((K, N), bf16),
        pltpu.VMEM((N, K), bf16),
        pltpu.VMEM((8, N), jnp.int32),
        pltpu.VMEM((R + H, D), bf16),
        pltpu.VMEM((R + H, D), bf16),
        pltpu.VMEM((H, D), bf16),
        pltpu.VMEM((H, D), bf16),
        pltpu.VMEM((H, S), bf16),
        pltpu.VMEM((R + H, S), f32),
        pltpu.VMEM((S, D + S), bf16),
        pltpu.VMEM((S, D), bf16),
        pltpu.VMEM((S, D + S), bf16),
        pltpu.VMEM((S, D), bf16),
        pltpu.VMEM((S, D), bf16),
        pltpu.VMEM((S, D), bf16),
        pltpu.VMEM((K, D), bf16),
        pltpu.VMEM((K, D), bf16),
        pltpu.VMEM((3, HALF, D), bf16),
        pltpu.VMEM((3, HALF, D), bf16),
        pltpu.VMEM((3, HALF, D), f32),
        pltpu.VMEM((3, HALF, D), bf16),
        pltpu.VMEM((3, 3, 3, 64, HALF), bf16),
        pltpu.VMEM((3, 3, 64, HALF), f32),
        pltpu.VMEM((3, 3, 64, HALF), bf16),
        pltpu.VMEM((3, 3, 3, 16, HALF), bf16),
        pltpu.VMEM((4, 3, 3, 16, HALF), bf16),
        pltpu.VMEM((3, D, D), bf16),
        dma((10,)),
        dma((4,)),
        dma((4,)),
        dma((3,)),
        dma((3,)),
        dma((3,)),
        dma((3,)),
        dma((3,)),
        dma((3,)),
        dma((3,)),
        dma((3,)),
        dma((3,)),
        dma((3,)),
        dma((3,)),
        dma((3,)),
        dma((3,)),
        dma((3,)),
    ]
    results = pl.pallas_call(
        kernel,
        out_shape=(
            pltpu.VMEM((N, D), bf16),
            pltpu.VMEM((N, D), bf16),
            pltpu.VMEM((D, D), f32),
            pltpu.VMEM((D, D), f32),
            pltpu.VMEM((D, D), f32),
        ),
        in_specs=[any_spec] * 8,
        out_specs=[vmem] * 5,
        scratch_shapes=scratch,
        compiler_params=pltpu.CompilerParams(
            collective_id=0, has_side_effects=True, vmem_limit_bytes=44 * 2**20
        ),
        name="layer",
    )(
        cells_in, w_in, w_edge, w_out, cotangent,
        cell_row.reshape(1, N), send_slot, recv_target,
    )
    outs = tuple(jax.ShapeDtypeStruct(r.shape, r.dtype) for r in results)
    return pl.pallas_call(
        write,
        out_shape=outs,
        in_specs=[any_spec] * 5,
        out_specs=[any_spec] * 5,
        scratch_shapes=[dma((5,))],
        compiler_params=pltpu.CompilerParams(vmem_limit_bytes=2**20),
        name="write",
    )(*results)


def solution(mesh):
    placed = (
        P(("cells", "edges"), None),
        P(),
        P(),
        P(),
        P(("cells", "edges"), None),
        P(("cells", "edges")),
        P(None, ("cells", "edges")),
        P(("cells", "edges"), None),
    )
    return jax.shard_map(
        per_device,
        mesh=mesh,
        in_specs=placed,
        out_specs=(P(("cells", "edges"), None), P(("cells", "edges"), None), P(), P(), P()),
        check_vma=False,
    )
```

```python
import jax
import jax.numpy as jnp
from jax import lax
from jax.experimental import pallas as pl
from jax.experimental.pallas import tpu as pltpu
from jax.sharding import PartitionSpec as P

N = 2048
D = 768
R = 256
H = 256
S = 128
CAP = 32
K = R + S
M = 1024
HALF = D // 2
WEDGE, WOUT, WIN = 0, 1, 2
BOTH = (0, 2)
LAST = (2, 1)

f32 = jnp.float32
bf16 = jnp.bfloat16
NT = (((1,), (1,)), ((), ()))
TN = (((0,), (0,)), ((), ()))


def dot(a, b):
    return jnp.dot(a, b, preferred_element_type=f32)


def dot_nt(a, b):
    return lax.dot_general(a, b, NT, preferred_element_type=f32)


def dot_tn(a, b):
    return lax.dot_general(a, b, TN, preferred_element_type=f32)


def aligned(x, m):
    return pl.multiple_of(x, m)


def kernel(
    cells_h, w_in_h, w_edge_h, w_out_h, cot_h, row_h, slot_h, tgt_h,
    mixed, gpre, win_ref, wedge_ref, wout_ref,
    row_ref, slot_ref, tgt_ref, cells, cot, w_in, w_edge, w_out, dact, hot_t,
    means, hgrads, hout, gmean, tgt_t, inv,
    out1, out3, got1, got3, reply2, reply4, cat2, cat4,
    send0, recv0, part, send_a, recv_a, part_b, send_b, recv_b, recv_c, fin,
    in_sem,
    x_ss, x_rs, p_ss, p_rs, a_ss, a_rs, b_ss, b_rs, c_ss, c_rs,
    bg_ss, bg_rs, ag_ss, ag_rs, pg_ss, pg_rs,
):
    ci = lax.axis_index("cells")
    x = lax.axis_index("edges")
    core = lax.rem(ci, 2)
    z = lax.rem(lax.div(ci, 2), 4)
    y = lax.div(ci, 8)

    def on_x(k):
        return {"cells": ci, "edges": lax.rem(x + k, 4)}

    def on_y(k):
        return {"cells": (lax.rem(y + k, 4) * 4 + z) * 2 + core, "edges": x}

    def on_z(k):
        return {"cells": (y * 4 + lax.rem(z + k, 4)) * 2 + core, "edges": x}

    twin = {"cells": ci + 1 - 2 * core, "edges": x}
    at = (x, y, z)
    peer = (on_x, on_y, on_z)

    msg, gmix = mixed, gpre

    loads = {}

    def arrive(name):
        loads.pop(name).wait()

    def load(name, src, dst, i):
        loads[name] = pltpu.make_async_copy(src, dst, in_sem.at[i])
        loads[name].start()

    for i, (name, src, dst) in enumerate(
        (
            ("rows", row_h, row_ref),
            ("slots", slot_h, slot_ref),
            ("targets", tgt_h, tgt_ref),
            ("w_in", w_in_h, w_in),
            ("cells0", cells_h.at[pl.ds(0, M)], cells.at[pl.ds(0, M)]),
            ("cells1", cells_h.at[pl.ds(M, M)], cells.at[pl.ds(M, M)]),
            ("w_out", w_out_h, w_out),
            ("cot0", cot_h.at[pl.ds(0, M)], cot.at[pl.ds(0, M)]),
            ("cot1", cot_h.at[pl.ds(M, M)], cot.at[pl.ds(M, M)]),
            ("w_edge", w_edge_h, w_edge),
        )
    ):
        load(name, src, dst, i)

    barrier = pltpu.get_barrier_semaphore()
    for k in (1, 2, 3):
        for where in peer:
            pl.semaphore_signal(
                barrier, inc=1, device_id=where(k), device_id_type=pl.DeviceIdType.MESH
            )
    pl.semaphore_signal(barrier, inc=1, device_id=twin, device_id_type=pl.DeviceIdType.MESH)

    sent = []

    def send(src, dst, ss, rs, where):
        pltpu.make_async_remote_copy(
            src_ref=src, dst_ref=dst, send_sem=ss, recv_sem=rs,
            device_id=where, device_id_type=pl.DeviceIdType.MESH,
        ).start()

    def take(ref, sem):
        pltpu.make_async_copy(ref, ref, sem).wait()

    for name in ("rows", "slots", "targets"):
        arrive(name)
    tgt_t[...] = (lax.broadcasted_iota(jnp.int32, (H, S), 0) == tgt_ref[...]).astype(bf16)

    def ones_where(mask):
        return jnp.where(mask, 1.0, 0.0)

    hot_t[0:R, :] = ones_where(
        lax.broadcasted_iota(jnp.int32, (R, N), 0) == row_ref[...]
    ).astype(bf16)
    slot_i = lax.broadcasted_iota(jnp.int32, (S, N), 0)
    hot_t[R:K, :] = (
        ones_where(slot_i == slot_ref[0:1, :]) + ones_where(slot_i == slot_ref[1:2, :])
    ).astype(bf16)
    arrive("w_in")
    for i in range(N // M):
        rows = pl.ds(i * M, M)
        arrive("cells%d" % i)
        pre = dot(cells[rows, :], w_in[...])
        sig = 0.5 * jnp.tanh(0.5 * pre) + 0.5
        m = pre * sig
        msg[rows, :] = m.astype(bf16)
        dact[rows, :] = (sig + m * (1.0 - sig)).astype(bf16)

    ones = jnp.ones((N, S), bf16)
    out1[:, 0:D] = dot(hot_t[R:K, :], msg[...]).astype(bf16)
    count = dot(hot_t[R:K, :], ones)
    high = jnp.floor(count * (1.0 / 128.0)) * 128.0
    lane = lax.broadcasted_iota(jnp.int32, (S, S), 1)
    out1[:, D:] = jnp.where(lane < S // 2, high, count - high).astype(bf16)

    pl.semaphore_wait(barrier, 10)

    def exchange(kind, src, dst, base):
        mine = pl.ds(aligned(base + x * CAP, CAP), CAP)
        for k in (2, 1, 3):
            theirs = pl.ds(aligned(lax.rem(x + k, 4) * CAP, CAP), CAP)
            send(src.at[theirs], dst.at[mine], x_ss.at[kind], x_rs.at[kind], on_x(k))
        sent.append((src.at[pl.ds(0, 3 * CAP)], x_ss.at[kind]))
        dst[mine, :] = src[pl.ds(aligned(x * CAP, CAP), CAP), :]

    def arrived(kind, dst):
        take(dst.at[pl.ds(0, 3 * CAP)], x_rs.at[kind])

    near = pl.ds(aligned(core * HALF, 128), HALF)
    far = pl.ds(aligned((1 - core) * HALF, 128), HALF)
    axes = ((0, 1, 2), (1, 2, 0), (2, 0, 1))

    def piece_a(base, t, a):
        return (
            pl.ds(aligned(base + t * 128 + lax.div(a, 2) * 64, 64), 64),
            pl.ds(aligned(lax.rem(a, 2) * HALF, 128), HALF),
        )

    def piece_b(base, t, a, b):
        return (
            pl.ds(aligned(base + t * 128 + lax.div(a, 2) * 64 + b * 16, 16), 16),
            pl.ds(aligned(lax.rem(a, 2) * HALF, 128), HALF),
        )

    def around(ax, k):
        return lax.rem(at[ax] + k, 4)

    def some(span):
        return pl.ds(span[0], span[1])

    def gradient(g, left, right):
        send0[g] = dot_tn(left[:, far], right[...]).astype(bf16)
        send(send0.at[g], recv0.at[g], p_ss.at[g], p_rs.at[g], twin)
        sent.append((send0.at[g], p_ss.at[g]))
        part[g] = dot_tn(left[:, near], right[...])

    def step_a(span):
        gs, q = some(span), span[0]
        for g in range(span[0], span[0] + span[1]):
            take(recv0.at[g], p_rs.at[g])
            send_a[g] = (part[g] + recv0[g].astype(f32)).astype(bf16)
        for k in (2, 1, 3):
            for t in range(3):
                ax = axes[t][0]
                r, c = piece_a(0, t, around(ax, k))
                send(send_a.at[gs, r, c], recv_a.at[k - 1, t, gs], a_ss.at[q], a_rs.at[q], peer[ax](k))
        sent.append((recv_a.at[:, :, gs], a_ss.at[q]))

    def step_b(span):
        gs, q = some(span), span[0]
        take(recv_a.at[:, :, gs], a_rs.at[q])
        for t in range(3):
            ax = axes[t][1]
            r, c = piece_a(0, t, at[axes[t][0]])
            total = part[gs, r, c] + recv0[gs, r, c].astype(f32)
            for k in range(3):
                total = total + recv_a[k, t, gs].astype(f32)
            part_b[t, gs] = total
            send_b[t, gs] = total.astype(bf16)
            for k in (2, 1, 3):
                theirs = pl.ds(aligned(around(ax, k) * 16, 16), 16)
                send(send_b.at[t, gs, theirs], recv_b.at[k - 1, t, gs], b_ss.at[q], b_rs.at[q], peer[ax](k))
        sent.append((recv_b.at[:, :, gs], b_ss.at[q]))

    def step_c(span):
        gs, q = some(span), span[0]
        take(recv_b.at[:, :, gs], b_rs.at[q])
        for t in range(3):
            ax = axes[t][2]
            mine = pl.ds(aligned(at[axes[t][1]] * 16, 16), 16)
            total = part_b[t, gs, mine, :]
            for k in range(3):
                total = total + recv_b[k, t, gs].astype(f32)
            recv_c[pl.ds(at[ax], 1), t, gs] = total.astype(bf16)[None]
            block = recv_c.at[at[ax], t, gs]
            for k in (2, 1, 3):
                send(block, block, c_ss.at[q], c_rs.at[q], peer[ax](k))
        sent.append((recv_b.at[:, :, gs], c_ss.at[q]))

    def gather_b(span):
        gs, q = some(span), span[0]
        take(recv_b.at[:, :, gs], c_rs.at[q])
        for t in range(3):
            ax = axes[t][1]
            total = recv_c[0, t, gs].astype(f32)
            for k in (1, 2, 3):
                total = total + recv_c[k, t, gs].astype(f32)
            r, c = piece_b(core * HALF, t, at[axes[t][0]], at[ax])
            fin[gs, r, c] = total.astype(bf16)
            block = fin.at[gs, r, c]
            for k in (2, 1, 3):
                send(block, block, bg_ss.at[q], bg_rs.at[q], peer[ax](k))
        sent.append((recv_b.at[:, :, gs], bg_ss.at[q]))

    def to_twin(span, t, a):
        r, c = piece_a(core * HALF, t, a)
        block = fin.at[some(span), r, c]
        send(block, block, pg_ss.at[span[0]], pg_rs.at[span[0]], twin)

    def gather_a(span):
        gs, q = some(span), span[0]
        take(recv_b.at[:, :, gs], bg_rs.at[q])
        for k in (1, 3, 2):
            for t in range(3):
                ax = axes[t][0]
                r, c = piece_a(core * HALF, t, at[ax])
                block = fin.at[gs, r, c]
                send(block, block, ag_ss.at[q], ag_rs.at[q, k - 1], peer[ax](k))
        sent.append((recv_a.at[:, :, gs], ag_ss.at[q]))
        for t in range(3):
            to_twin(span, t, at[axes[t][0]])
        sent.append((fin.at[gs, near], pg_ss.at[q]))

    def gather_p(span, k):
        take(recv_a.at[k - 1, :, some(span)], ag_rs.at[span[0], k - 1])
        for t in range(3):
            to_twin(span, t, around(axes[t][0], 4 - k))

    def all_sent():
        for ref, sem in sent:
            take(ref, sem)
        sent.clear()

    def finish_near(span, *outs):
        for g, out in enumerate(outs, span[0]):
            out[near, :] = fin[g, near, :].astype(f32)

    def finish_far(span, *outs):
        take(fin.at[some(span), far], pg_rs.at[span[0]])
        for g, out in enumerate(outs, span[0]):
            out[far, :] = fin[g, far, :].astype(f32)

    def grad_mixed(i):
        rows = pl.ds(i * M, M)
        arrive("cot%d" % i)
        gmix[rows, :] = dot_nt(cot[rows, :], w_out[...]).astype(bf16)

    exchange(0, out1, got1, 0)
    inv[0:R, :] = 1.0 / (dot(hot_t[0:R, :], ones) + 1.0)
    means[0:R, :] = (dot(hot_t[0:R, :], msg[...]) * inv[0:R, 0:1]).astype(bf16)
    arrive("w_out")
    grad_mixed(0)
    arrive("w_edge")
    arrived(0, got1)
    counted = dot(tgt_t[...], got1[:, D:])
    inv[R:, :] = jnp.broadcast_to(
        1.0 / (counted[:, 0:1] + counted[:, S // 2 : S // 2 + 1] + 1.0), (H, S)
    )
    means[R:, :] = (dot(tgt_t[...], got1[:, 0:D]) * inv[R:, 0:1]).astype(bf16)
    hout[...] = dot(means[R:, :], w_edge[...]).astype(bf16)
    reply2[...] = dot_tn(tgt_t[...], hout[...]).astype(bf16)
    exchange(2, reply2, cat2, R)
    grad_mixed(1)
    out3[...] = dot(hot_t[R:K, :], gmix[...]).astype(bf16)
    exchange(1, out3, got3, 0)
    cat2[0:R, :] = dot(means[0:R, :], w_edge[...]).astype(bf16)
    arrived(2, cat2)
    for i in range(N // M):
        rows = pl.ds(i * M, M)
        mixed[rows, :] = dot_tn(hot_t[:, rows], cat2[...]).astype(bf16)
    gradient(WOUT, mixed, cot)
    arrived(1, got3)
    hgrads[R:, :] = dot(tgt_t[...], got3[...]).astype(bf16)
    gmean[...] = (dot_nt(hgrads[R:, :], w_edge[...]) * inv[R:, 0:1]).astype(bf16)
    reply4[...] = dot_tn(tgt_t[...], gmean[...]).astype(bf16)
    exchange(3, reply4, cat4, R)
    hgrads[0:R, :] = dot(hot_t[0:R, :], gmix[...]).astype(bf16)
    cat4[0:R, :] = (dot_nt(hgrads[0:R, :], w_edge[...]) * inv[0:R, 0:1]).astype(bf16)
    gradient(WEDGE, means, hgrads)
    arrived(3, cat4)
    for i in range(N // M):
        rows = pl.ds(i * M, M)
        gpre[rows, :] = (dot_tn(hot_t[:, rows], cat4[...]) * dact[rows, :].astype(f32)).astype(bf16)
        if i == 0:
            step_a(BOTH)
    gradient(WIN, cells, gpre)
    step_a(LAST)

    def layer_out(i):
        rows = pl.ds(i * M, M)
        mixed[rows, :] = (cells[rows, :].astype(f32) + dot(mixed[rows, :], w_out[...])).astype(bf16)

    def grad_cells(start, n):
        rows = pl.ds(start, n)
        gpre[rows, :] = (cot[rows, :].astype(f32) + dot_nt(gpre[rows, :], w_in[...])).astype(bf16)

    layer_out(0)
    step_b(BOTH)
    layer_out(1)
    step_b(LAST)
    grad_cells(0, M)
    step_c(BOTH)
    grad_cells(M, M // 2)
    step_c(LAST)
    grad_cells(M + M // 2, M // 2)
    all_sent()
    gather_b(BOTH)
    gather_b(LAST)
    gather_a(BOTH)
    gather_a(LAST)
    for span in (BOTH, LAST):
        for k in (1, 3, 2):
            gather_p(span, k)
    finish_near(BOTH, wedge_ref, wout_ref)
    finish_near(LAST, win_ref)
    finish_far(BOTH, wedge_ref, wout_ref)
    finish_far(LAST, win_ref)
    all_sent()


def write(*refs):
    n = len(refs) // 2
    copies = [
        pltpu.make_async_copy(refs[i], refs[n + i], refs[2 * n].at[i]) for i in range(n)
    ]
    for copy in copies:
        copy.start()
    for copy in copies:
        copy.wait()


def per_device(cells_in, w_in, w_edge, w_out, cotangent, cell_row, send_slot, recv_target):
    any_spec = pl.BlockSpec(memory_space=pl.ANY)
    vmem = pl.BlockSpec(memory_space=pltpu.VMEM)
    dma = pltpu.SemaphoreType.DMA
    scratch = [
        pltpu.VMEM((1, N), jnp.int32),
        pltpu.VMEM((2, N), jnp.int32),
        pltpu.VMEM((1, S), jnp.int32),
        pltpu.VMEM((N, D), bf16),
        pltpu.VMEM((N, D), bf16),
        pltpu.VMEM((D, D), bf16),
        pltpu.VMEM((D, D), bf16),
        pltpu.VMEM((D, D), bf16),
        pltpu.VMEM((N, D), bf16),
        pltpu.VMEM((K, N), bf16),
        pltpu.VMEM((R + H, D), bf16),
        pltpu.VMEM((R + H, D), bf16),
        pltpu.VMEM((H, D), bf16),
        pltpu.VMEM((H, D), bf16),
        pltpu.VMEM((H, S), bf16),
        pltpu.VMEM((R + H, S), f32),
        pltpu.VMEM((S, D + S), bf16),
        pltpu.VMEM((S, D), bf16),
        pltpu.VMEM((S, D + S), bf16),
        pltpu.VMEM((S, D), bf16),
        pltpu.VMEM((S, D), bf16),
        pltpu.VMEM((S, D), bf16),
        pltpu.VMEM((K, D), bf16),
        pltpu.VMEM((K, D), bf16),
        pltpu.VMEM((3, HALF, D), bf16),
        pltpu.VMEM((3, HALF, D), bf16),
        pltpu.VMEM((3, HALF, D), f32),
        pltpu.VMEM((3, HALF, D), bf16),
        pltpu.VMEM((3, 3, 3, 64, HALF), bf16),
        pltpu.VMEM((3, 3, 64, HALF), f32),
        pltpu.VMEM((3, 3, 64, HALF), bf16),
        pltpu.VMEM((3, 3, 3, 16, HALF), bf16),
        pltpu.VMEM((4, 3, 3, 16, HALF), bf16),
        pltpu.VMEM((3, D, D), bf16),
        dma((10,)),
        dma((4,)),
        dma((4,)),
        dma((3,)),
        dma((3,)),
        dma((3,)),
        dma((3,)),
        dma((3,)),
        dma((3,)),
        dma((3,)),
        dma((3,)),
        dma((3,)),
        dma((3,)),
        dma((3,)),
        dma((3, 3)),
        dma((3,)),
        dma((3,)),
    ]
    results = pl.pallas_call(
        kernel,
        out_shape=(
            pltpu.VMEM((N, D), bf16),
            pltpu.VMEM((N, D), bf16),
            pltpu.VMEM((D, D), f32),
            pltpu.VMEM((D, D), f32),
            pltpu.VMEM((D, D), f32),
        ),
        in_specs=[any_spec] * 8,
        out_specs=[vmem] * 5,
        scratch_shapes=scratch,
        compiler_params=pltpu.CompilerParams(
            collective_id=0, has_side_effects=True, vmem_limit_bytes=44 * 2**20
        ),
        name="layer",
    )(
        cells_in, w_in, w_edge, w_out, cotangent,
        cell_row.reshape(1, N), send_slot, recv_target,
    )
    outs = tuple(jax.ShapeDtypeStruct(r.shape, r.dtype) for r in results)
    return pl.pallas_call(
        write,
        out_shape=outs,
        in_specs=[any_spec] * 5,
        out_specs=[any_spec] * 5,
        scratch_shapes=[dma((5,))],
        compiler_params=pltpu.CompilerParams(vmem_limit_bytes=2**20),
        name="write",
    )(*results)


def solution(mesh):
    placed = (
        P(("cells", "edges"), None),
        P(),
        P(),
        P(),
        P(("cells", "edges"), None),
        P(("cells", "edges")),
        P(None, ("cells", "edges")),
        P(("cells", "edges"), None),
    )
    return jax.shard_map(
        per_device,
        mesh=mesh,
        in_specs=placed,
        out_specs=(P(("cells", "edges"), None), P(("cells", "edges"), None), P(), P(), P()),
        check_vma=False,
    )
```

```python
import jax
import jax.numpy as jnp
from jax import lax
from jax.experimental import pallas as pl
from jax.experimental.pallas import tpu as pltpu
from jax.sharding import PartitionSpec as P

N = 2048
D = 768
R = 256
H = 256
S = 128
CAP = 32
K = R + S
M = 1024
HALF = D // 2
WEDGE, WOUT, WIN = 0, 1, 2
BOTH = (0, 2)
LAST = (2, 1)

f32 = jnp.float32
bf16 = jnp.bfloat16
NT = (((1,), (1,)), ((), ()))
TN = (((0,), (0,)), ((), ()))


def dot(a, b):
    return jnp.dot(a, b, preferred_element_type=f32)


def dot_nt(a, b):
    return lax.dot_general(a, b, NT, preferred_element_type=f32)


def dot_tn(a, b):
    return lax.dot_general(a, b, TN, preferred_element_type=f32)


def aligned(x, m):
    return pl.multiple_of(x, m)


def kernel(
    cells_h, w_in_h, w_edge_h, w_out_h, cot_h, row_h, slot_h, tgt_h,
    mixed, gpre, win_ref, wedge_ref, wout_ref,
    row_ref, slot_ref, tgt_ref, cells, cot, w_in, w_edge, w_out, dact, hot_t,
    means, hgrads, hout, gmean, tgt_t, inv,
    out1, out3, got1, got3, reply2, reply4, cat2, cat4,
    send0, recv0, part, send_a, recv_a, part_b, send_b, recv_b, recv_c, fin,
    in_sem,
    x_ss, x_rs, p_ss, p_rs, a_ss, a_rs, b_ss, b_rs, c_ss, c_rs,
    bg_ss, bg_rs, ag_ss, ag_rs, pg_ss, pg_rs,
):
    ci = lax.axis_index("cells")
    x = lax.axis_index("edges")
    core = lax.rem(ci, 2)
    z = lax.rem(lax.div(ci, 2), 4)
    y = lax.div(ci, 8)

    def on_x(k):
        return {"cells": ci, "edges": lax.rem(x + k, 4)}

    def on_y(k):
        return {"cells": (lax.rem(y + k, 4) * 4 + z) * 2 + core, "edges": x}

    def on_z(k):
        return {"cells": (y * 4 + lax.rem(z + k, 4)) * 2 + core, "edges": x}

    twin = {"cells": ci + 1 - 2 * core, "edges": x}
    at = (x, y, z)
    peer = (on_x, on_y, on_z)

    msg, gmix = mixed, gpre

    loads = {}

    def arrive(name):
        loads.pop(name).wait()

    def load(name, src, dst, i):
        loads[name] = pltpu.make_async_copy(src, dst, in_sem.at[i])
        loads[name].start()

    for i, (name, src, dst) in enumerate(
        (
            ("rows", row_h, row_ref),
            ("slots", slot_h, slot_ref),
            ("targets", tgt_h, tgt_ref),
            ("w_in", w_in_h, w_in),
            ("cells0", cells_h.at[pl.ds(0, M)], cells.at[pl.ds(0, M)]),
            ("cells1", cells_h.at[pl.ds(M, M)], cells.at[pl.ds(M, M)]),
            ("w_out", w_out_h, w_out),
            ("cot0", cot_h.at[pl.ds(0, M)], cot.at[pl.ds(0, M)]),
            ("cot1", cot_h.at[pl.ds(M, M)], cot.at[pl.ds(M, M)]),
            ("w_edge", w_edge_h, w_edge),
        )
    ):
        load(name, src, dst, i)

    barrier = pltpu.get_barrier_semaphore()
    for k in (1, 2, 3):
        for where in peer:
            pl.semaphore_signal(
                barrier, inc=1, device_id=where(k), device_id_type=pl.DeviceIdType.MESH
            )
    pl.semaphore_signal(barrier, inc=1, device_id=twin, device_id_type=pl.DeviceIdType.MESH)

    sent = []

    def send(src, dst, ss, rs, where):
        pltpu.make_async_remote_copy(
            src_ref=src, dst_ref=dst, send_sem=ss, recv_sem=rs,
            device_id=where, device_id_type=pl.DeviceIdType.MESH,
        ).start()

    def take(ref, sem):
        pltpu.make_async_copy(ref, ref, sem).wait()

    for name in ("rows", "slots", "targets"):
        arrive(name)
    tgt_t[...] = (lax.broadcasted_iota(jnp.int32, (H, S), 0) == tgt_ref[...]).astype(bf16)

    def ones_where(mask):
        return jnp.where(mask, 1.0, 0.0)

    hot_t[0:R, :] = ones_where(
        lax.broadcasted_iota(jnp.int32, (R, N), 0) == row_ref[...]
    ).astype(bf16)
    slot_i = lax.broadcasted_iota(jnp.int32, (S, N), 0)
    hot_t[R:K, :] = (
        ones_where(slot_i == slot_ref[0:1, :]) + ones_where(slot_i == slot_ref[1:2, :])
    ).astype(bf16)
    arrive("w_in")
    for i in range(N // M):
        rows = pl.ds(i * M, M)
        arrive("cells%d" % i)
        pre = dot(cells[rows, :], w_in[...])
        sig = 0.5 * jnp.tanh(0.5 * pre) + 0.5
        m = pre * sig
        msg[rows, :] = m.astype(bf16)
        dact[rows, :] = (sig + m * (1.0 - sig)).astype(bf16)

    ones = jnp.ones((N, S), bf16)
    out1[:, 0:D] = dot(hot_t[R:K, :], msg[...]).astype(bf16)
    count = dot(hot_t[R:K, :], ones)
    high = jnp.floor(count * (1.0 / 128.0)) * 128.0
    lane = lax.broadcasted_iota(jnp.int32, (S, S), 1)
    out1[:, D:] = jnp.where(lane < S // 2, high, count - high).astype(bf16)

    pl.semaphore_wait(barrier, 10)

    def exchange(kind, src, dst, base):
        mine = pl.ds(aligned(base + x * CAP, CAP), CAP)
        for k in (2, 1, 3):
            theirs = pl.ds(aligned(lax.rem(x + k, 4) * CAP, CAP), CAP)
            send(src.at[theirs], dst.at[mine], x_ss.at[kind], x_rs.at[kind], on_x(k))
        sent.append((src.at[pl.ds(0, 3 * CAP)], x_ss.at[kind]))
        dst[mine, :] = src[pl.ds(aligned(x * CAP, CAP), CAP), :]

    def arrived(kind, dst):
        take(dst.at[pl.ds(0, 3 * CAP)], x_rs.at[kind])

    near = pl.ds(aligned(core * HALF, 128), HALF)
    far = pl.ds(aligned((1 - core) * HALF, 128), HALF)
    axes = ((0, 1, 2), (1, 2, 0), (2, 0, 1))

    def piece_a(base, t, a):
        return (
            pl.ds(aligned(base + t * 128 + lax.div(a, 2) * 64, 64), 64),
            pl.ds(aligned(lax.rem(a, 2) * HALF, 128), HALF),
        )

    def piece_b(base, t, a, b):
        return (
            pl.ds(aligned(base + t * 128 + lax.div(a, 2) * 64 + b * 16, 16), 16),
            pl.ds(aligned(lax.rem(a, 2) * HALF, 128), HALF),
        )

    def around(ax, k):
        return lax.rem(at[ax] + k, 4)

    def some(span):
        return pl.ds(span[0], span[1])

    def gradient(g, left, right):
        send0[g] = dot_tn(left[:, far], right[...]).astype(bf16)
        send(send0.at[g], recv0.at[g], p_ss.at[g], p_rs.at[g], twin)
        sent.append((send0.at[g], p_ss.at[g]))
        part[g] = dot_tn(left[:, near], right[...])

    def step_a(span):
        gs, q = some(span), span[0]
        for g in range(span[0], span[0] + span[1]):
            take(recv0.at[g], p_rs.at[g])
            send_a[g] = (part[g] + recv0[g].astype(f32)).astype(bf16)
        for k in (2, 1, 3):
            for t in range(3):
                ax = axes[t][0]
                r, c = piece_a(0, t, around(ax, k))
                send(send_a.at[gs, r, c], recv_a.at[k - 1, t, gs], a_ss.at[q], a_rs.at[q], peer[ax](k))
        sent.append((recv_a.at[:, :, gs], a_ss.at[q]))

    def step_b(span):
        gs, q = some(span), span[0]
        take(recv_a.at[:, :, gs], a_rs.at[q])
        for t in range(3):
            ax = axes[t][1]
            r, c = piece_a(0, t, at[axes[t][0]])
            total = part[gs, r, c] + recv0[gs, r, c].astype(f32)
            for k in range(3):
                total = total + recv_a[k, t, gs].astype(f32)
            part_b[t, gs] = total
            send_b[t, gs] = total.astype(bf16)
            for k in (2, 1, 3):
                theirs = pl.ds(aligned(around(ax, k) * 16, 16), 16)
                send(send_b.at[t, gs, theirs], recv_b.at[k - 1, t, gs], b_ss.at[q], b_rs.at[q], peer[ax](k))
        sent.append((recv_b.at[:, :, gs], b_ss.at[q]))

    def step_c(span):
        gs, q = some(span), span[0]
        take(recv_b.at[:, :, gs], b_rs.at[q])
        for t in range(3):
            ax = axes[t][2]
            mine = pl.ds(aligned(at[axes[t][1]] * 16, 16), 16)
            total = part_b[t, gs, mine, :]
            for k in range(3):
                total = total + recv_b[k, t, gs].astype(f32)
            recv_c[pl.ds(at[ax], 1), t, gs] = total.astype(bf16)[None]
            block = recv_c.at[at[ax], t, gs]
            for k in (2, 1, 3):
                send(block, block, c_ss.at[q], c_rs.at[q], peer[ax](k))
        sent.append((recv_b.at[:, :, gs], c_ss.at[q]))

    def gather_b(span):
        gs, q = some(span), span[0]
        take(recv_b.at[:, :, gs], c_rs.at[q])
        for t in range(3):
            ax = axes[t][1]
            total = recv_c[0, t, gs].astype(f32)
            for k in (1, 2, 3):
                total = total + recv_c[k, t, gs].astype(f32)
            r, c = piece_b(core * HALF, t, at[axes[t][0]], at[ax])
            fin[gs, r, c] = total.astype(bf16)
            block = fin.at[gs, r, c]
            for k in (2, 1, 3):
                send(block, block, bg_ss.at[q], bg_rs.at[q], peer[ax](k))
        sent.append((recv_b.at[:, :, gs], bg_ss.at[q]))

    def to_twin(span, t, a):
        r, c = piece_a(core * HALF, t, a)
        block = fin.at[some(span), r, c]
        send(block, block, pg_ss.at[span[0]], pg_rs.at[span[0]], twin)

    def gather_a(span):
        gs, q = some(span), span[0]
        take(recv_b.at[:, :, gs], bg_rs.at[q])
        for k in (1, 3, 2):
            for t in range(3):
                ax = axes[t][0]
                r, c = piece_a(core * HALF, t, at[ax])
                block = fin.at[gs, r, c]
                send(block, block, ag_ss.at[q], ag_rs.at[q, k - 1], peer[ax](k))
        sent.append((recv_a.at[:, :, gs], ag_ss.at[q]))
        for t in range(3):
            to_twin(span, t, at[axes[t][0]])
        sent.append((fin.at[gs, near], pg_ss.at[q]))

    def gather_p(span, k):
        take(recv_a.at[k - 1, :, some(span)], ag_rs.at[span[0], k - 1])
        for t in range(3):
            to_twin(span, t, around(axes[t][0], 4 - k))

    def all_sent():
        for ref, sem in sent:
            take(ref, sem)
        sent.clear()

    def finish_near(span, *outs):
        for g, out in enumerate(outs, span[0]):
            out[near, :] = fin[g, near, :].astype(f32)

    def finish_far(span, *outs):
        take(fin.at[some(span), far], pg_rs.at[span[0]])
        for g, out in enumerate(outs, span[0]):
            out[far, :] = fin[g, far, :].astype(f32)

    def grad_mixed(i):
        rows = pl.ds(i * M, M)
        arrive("cot%d" % i)
        gmix[rows, :] = dot_nt(cot[rows, :], w_out[...]).astype(bf16)

    exchange(0, out1, got1, 0)
    arrive("w_out")
    grad_mixed(0)
    grad_mixed(1)
    out3[...] = dot(hot_t[R:K, :], gmix[...]).astype(bf16)
    exchange(1, out3, got3, 0)
    arrive("w_edge")
    inv[0:R, :] = 1.0 / (dot(hot_t[0:R, :], ones) + 1.0)
    means[0:R, :] = (dot(hot_t[0:R, :], msg[...]) * inv[0:R, 0:1]).astype(bf16)
    arrived(0, got1)
    counted = dot(tgt_t[...], got1[:, D:])
    inv[R:, :] = jnp.broadcast_to(
        1.0 / (counted[:, 0:1] + counted[:, S // 2 : S // 2 + 1] + 1.0), (H, S)
    )
    means[R:, :] = (dot(tgt_t[...], got1[:, 0:D]) * inv[R:, 0:1]).astype(bf16)
    hout[...] = dot(means[R:, :], w_edge[...]).astype(bf16)
    reply2[...] = dot_tn(tgt_t[...], hout[...]).astype(bf16)
    exchange(2, reply2, cat2, R)
    cat2[0:R, :] = dot(means[0:R, :], w_edge[...]).astype(bf16)
    hgrads[0:R, :] = dot(hot_t[0:R, :], gmix[...]).astype(bf16)
    arrived(1, got3)
    hgrads[R:, :] = dot(tgt_t[...], got3[...]).astype(bf16)
    gmean[...] = (dot_nt(hgrads[R:, :], w_edge[...]) * inv[R:, 0:1]).astype(bf16)
    reply4[...] = dot_tn(tgt_t[...], gmean[...]).astype(bf16)
    exchange(3, reply4, cat4, R)
    cat4[0:R, :] = (dot_nt(hgrads[0:R, :], w_edge[...]) * inv[0:R, 0:1]).astype(bf16)
    gradient(WEDGE, means, hgrads)
    arrived(2, cat2)
    for i in range(N // M):
        rows = pl.ds(i * M, M)
        mixed[rows, :] = dot_tn(hot_t[:, rows], cat2[...]).astype(bf16)
    gradient(WOUT, mixed, cot)
    arrived(3, cat4)
    for i in range(N // M):
        rows = pl.ds(i * M, M)
        gpre[rows, :] = (dot_tn(hot_t[:, rows], cat4[...]) * dact[rows, :].astype(f32)).astype(bf16)
    step_a(BOTH)
    gradient(WIN, cells, gpre)
    step_a(LAST)

    def layer_out(i):
        rows = pl.ds(i * M, M)
        mixed[rows, :] = (cells[rows, :].astype(f32) + dot(mixed[rows, :], w_out[...])).astype(bf16)

    def grad_cells(start, n):
        rows = pl.ds(start, n)
        gpre[rows, :] = (cot[rows, :].astype(f32) + dot_nt(gpre[rows, :], w_in[...])).astype(bf16)

    layer_out(0)
    step_b(BOTH)
    layer_out(1)
    step_b(LAST)
    grad_cells(0, M)
    step_c(BOTH)
    grad_cells(M, M // 2)
    step_c(LAST)
    grad_cells(M + M // 2, M // 2)
    all_sent()
    gather_b(BOTH)
    gather_b(LAST)
    gather_a(BOTH)
    gather_a(LAST)
    for span in (BOTH, LAST):
        for k in (1, 3, 2):
            gather_p(span, k)
    finish_near(BOTH, wedge_ref, wout_ref)
    finish_near(LAST, win_ref)
    finish_far(BOTH, wedge_ref, wout_ref)
    finish_far(LAST, win_ref)
    all_sent()


def write(*refs):
    n = len(refs) // 2
    copies = [
        pltpu.make_async_copy(refs[i], refs[n + i], refs[2 * n].at[i]) for i in range(n)
    ]
    for copy in copies:
        copy.start()
    for copy in copies:
        copy.wait()


def per_device(cells_in, w_in, w_edge, w_out, cotangent, cell_row, send_slot, recv_target):
    any_spec = pl.BlockSpec(memory_space=pl.ANY)
    vmem = pl.BlockSpec(memory_space=pltpu.VMEM)
    dma = pltpu.SemaphoreType.DMA
    scratch = [
        pltpu.VMEM((1, N), jnp.int32),
        pltpu.VMEM((2, N), jnp.int32),
        pltpu.VMEM((1, S), jnp.int32),
        pltpu.VMEM((N, D), bf16),
        pltpu.VMEM((N, D), bf16),
        pltpu.VMEM((D, D), bf16),
        pltpu.VMEM((D, D), bf16),
        pltpu.VMEM((D, D), bf16),
        pltpu.VMEM((N, D), bf16),
        pltpu.VMEM((K, N), bf16),
        pltpu.VMEM((R + H, D), bf16),
        pltpu.VMEM((R + H, D), bf16),
        pltpu.VMEM((H, D), bf16),
        pltpu.VMEM((H, D), bf16),
        pltpu.VMEM((H, S), bf16),
        pltpu.VMEM((R + H, S), f32),
        pltpu.VMEM((S, D + S), bf16),
        pltpu.VMEM((S, D), bf16),
        pltpu.VMEM((S, D + S), bf16),
        pltpu.VMEM((S, D), bf16),
        pltpu.VMEM((S, D), bf16),
        pltpu.VMEM((S, D), bf16),
        pltpu.VMEM((K, D), bf16),
        pltpu.VMEM((K, D), bf16),
        pltpu.VMEM((3, HALF, D), bf16),
        pltpu.VMEM((3, HALF, D), bf16),
        pltpu.VMEM((3, HALF, D), f32),
        pltpu.VMEM((3, HALF, D), bf16),
        pltpu.VMEM((3, 3, 3, 64, HALF), bf16),
        pltpu.VMEM((3, 3, 64, HALF), f32),
        pltpu.VMEM((3, 3, 64, HALF), bf16),
        pltpu.VMEM((3, 3, 3, 16, HALF), bf16),
        pltpu.VMEM((4, 3, 3, 16, HALF), bf16),
        pltpu.VMEM((3, D, D), bf16),
        dma((10,)),
        dma((4,)),
        dma((4,)),
        dma((3,)),
        dma((3,)),
        dma((3,)),
        dma((3,)),
        dma((3,)),
        dma((3,)),
        dma((3,)),
        dma((3,)),
        dma((3,)),
        dma((3,)),
        dma((3,)),
        dma((3, 3)),
        dma((3,)),
        dma((3,)),
    ]
    results = pl.pallas_call(
        kernel,
        out_shape=(
            pltpu.VMEM((N, D), bf16),
            pltpu.VMEM((N, D), bf16),
            pltpu.VMEM((D, D), f32),
            pltpu.VMEM((D, D), f32),
            pltpu.VMEM((D, D), f32),
        ),
        in_specs=[any_spec] * 8,
        out_specs=[vmem] * 5,
        scratch_shapes=scratch,
        compiler_params=pltpu.CompilerParams(
            collective_id=0, has_side_effects=True, vmem_limit_bytes=44 * 2**20
        ),
        name="layer",
    )(
        cells_in, w_in, w_edge, w_out, cotangent,
        cell_row.reshape(1, N), send_slot, recv_target,
    )
    outs = tuple(jax.ShapeDtypeStruct(r.shape, r.dtype) for r in results)
    return pl.pallas_call(
        write,
        out_shape=outs,
        in_specs=[any_spec] * 5,
        out_specs=[any_spec] * 5,
        scratch_shapes=[dma((5,))],
        compiler_params=pltpu.CompilerParams(vmem_limit_bytes=2**20),
        name="write",
    )(*results)


def solution(mesh):
    placed = (
        P(("cells", "edges"), None),
        P(),
        P(),
        P(),
        P(("cells", "edges"), None),
        P(("cells", "edges")),
        P(None, ("cells", "edges")),
        P(("cells", "edges"), None),
    )
    return jax.shard_map(
        per_device,
        mesh=mesh,
        in_specs=placed,
        out_specs=(P(("cells", "edges"), None), P(("cells", "edges"), None), P(), P(), P()),
        check_vma=False,
    )
```

```python
import jax
import jax.numpy as jnp
from jax import lax
from jax.experimental import pallas as pl
from jax.experimental.pallas import tpu as pltpu
from jax.sharding import PartitionSpec as P

N = 2048
D = 768
R = 256
H = 256
S = 128
CAP = 32
K = R + S
M = 1024
HALF = D // 2
WEDGE, WOUT, WIN = 0, 1, 2
BOTH = (0, 2)
LAST = (2, 1)

f32 = jnp.float32
bf16 = jnp.bfloat16
NT = (((1,), (1,)), ((), ()))
TN = (((0,), (0,)), ((), ()))


def dot(a, b):
    return jnp.dot(a, b, preferred_element_type=f32)


def dot_nt(a, b):
    return lax.dot_general(a, b, NT, preferred_element_type=f32)


def dot_tn(a, b):
    return lax.dot_general(a, b, TN, preferred_element_type=f32)


def aligned(x, m):
    return pl.multiple_of(x, m)


def kernel(
    cells_h, w_in_h, w_edge_h, w_out_h, cot_h, row_h, slot_h, tgt_h,
    mixed, gpre, win_ref, wedge_ref, wout_ref,
    row_ref, slot_ref, tgt_ref, cells, cot, w_in, w_edge, w_out, dact, hot_t,
    means, hgrads, hout, gmean, tgt_t, inv,
    out1, out3, got1, got3, reply2, reply4, cat2, cat4,
    send0, recv0, part, send_a, recv_a, part_b, send_b, recv_b, recv_c, fin,
    in_sem,
    x_ss, x_rs, p_ss, p_rs, a_ss, a_rs, b_ss, b_rs, c_ss, c_rs,
    bg_ss, bg_rs, ag_ss, ag_rs, pg_ss, pg_rs,
):
    ci = lax.axis_index("cells")
    x = lax.axis_index("edges")
    core = lax.rem(ci, 2)
    z = lax.rem(lax.div(ci, 2), 4)
    y = lax.div(ci, 8)

    def on_x(k):
        return {"cells": ci, "edges": lax.rem(x + k, 4)}

    def on_y(k):
        return {"cells": (lax.rem(y + k, 4) * 4 + z) * 2 + core, "edges": x}

    def on_z(k):
        return {"cells": (y * 4 + lax.rem(z + k, 4)) * 2 + core, "edges": x}

    twin = {"cells": ci + 1 - 2 * core, "edges": x}
    at = (x, y, z)
    peer = (on_x, on_y, on_z)

    msg, gmix = mixed, gpre

    loads = {}

    def arrive(name):
        loads.pop(name).wait()

    def load(name, src, dst, i):
        loads[name] = pltpu.make_async_copy(src, dst, in_sem.at[i])
        loads[name].start()

    for i, (name, src, dst) in enumerate(
        (
            ("rows", row_h, row_ref),
            ("slots", slot_h, slot_ref),
            ("targets", tgt_h, tgt_ref),
            ("w_in", w_in_h, w_in),
            ("cells0", cells_h.at[pl.ds(0, M)], cells.at[pl.ds(0, M)]),
            ("cells1", cells_h.at[pl.ds(M, M)], cells.at[pl.ds(M, M)]),
            ("w_out", w_out_h, w_out),
            ("cot0", cot_h.at[pl.ds(0, M)], cot.at[pl.ds(0, M)]),
            ("cot1", cot_h.at[pl.ds(M, M)], cot.at[pl.ds(M, M)]),
            ("w_edge", w_edge_h, w_edge),
        )
    ):
        load(name, src, dst, i)

    barrier = pltpu.get_barrier_semaphore()
    for k in (1, 2, 3):
        for where in peer:
            pl.semaphore_signal(
                barrier, inc=1, device_id=where(k), device_id_type=pl.DeviceIdType.MESH
            )
    pl.semaphore_signal(barrier, inc=1, device_id=twin, device_id_type=pl.DeviceIdType.MESH)

    sent = []

    def send(src, dst, ss, rs, where):
        pltpu.make_async_remote_copy(
            src_ref=src, dst_ref=dst, send_sem=ss, recv_sem=rs,
            device_id=where, device_id_type=pl.DeviceIdType.MESH,
        ).start()

    def take(ref, sem):
        pltpu.make_async_copy(ref, ref, sem).wait()

    for name in ("rows", "slots", "targets"):
        arrive(name)
    tgt_t[...] = (lax.broadcasted_iota(jnp.int32, (H, S), 0) == tgt_ref[...]).astype(bf16)

    def ones_where(mask):
        return jnp.where(mask, 1.0, 0.0)

    hot_t[0:R, :] = ones_where(
        lax.broadcasted_iota(jnp.int32, (R, N), 0) == row_ref[...]
    ).astype(bf16)
    slot_i = lax.broadcasted_iota(jnp.int32, (S, N), 0)
    hot_t[R:K, :] = (
        ones_where(slot_i == slot_ref[0:1, :]) + ones_where(slot_i == slot_ref[1:2, :])
    ).astype(bf16)
    ones = jnp.ones((N, S), bf16)
    inv[0:R, :] = 1.0 / (dot(hot_t[0:R, :], ones) + 1.0)
    count = dot(hot_t[R:K, :], ones)
    high = jnp.floor(count * (1.0 / 128.0)) * 128.0
    lane = lax.broadcasted_iota(jnp.int32, (S, S), 1)
    out1[:, D:] = jnp.where(lane < S // 2, high, count - high).astype(bf16)
    arrive("w_in")
    for i in range(N // M):
        rows = pl.ds(i * M, M)
        arrive("cells%d" % i)
        pre = dot(cells[rows, :], w_in[...])
        sig = 0.5 * jnp.tanh(0.5 * pre) + 0.5
        m = pre * sig
        msg[rows, :] = m.astype(bf16)
        dact[rows, :] = (sig + m * (1.0 - sig)).astype(bf16)

    out1[:, 0:D] = dot(hot_t[R:K, :], msg[...]).astype(bf16)
    pl.semaphore_wait(barrier, 10)

    def exchange(kind, src, dst, base):
        mine = pl.ds(aligned(base + x * CAP, CAP), CAP)
        for k in (2, 1, 3):
            theirs = pl.ds(aligned(lax.rem(x + k, 4) * CAP, CAP), CAP)
            send(src.at[theirs], dst.at[mine], x_ss.at[kind], x_rs.at[kind], on_x(k))
        sent.append((src.at[pl.ds(0, 3 * CAP)], x_ss.at[kind]))
        dst[mine, :] = src[pl.ds(aligned(x * CAP, CAP), CAP), :]

    def arrived(kind, dst):
        take(dst.at[pl.ds(0, 3 * CAP)], x_rs.at[kind])

    near = pl.ds(aligned(core * HALF, 128), HALF)
    far = pl.ds(aligned((1 - core) * HALF, 128), HALF)
    axes = ((0, 1, 2), (1, 2, 0), (2, 0, 1))

    def piece_a(base, t, a):
        return (
            pl.ds(aligned(base + t * 128 + lax.div(a, 2) * 64, 64), 64),
            pl.ds(aligned(lax.rem(a, 2) * HALF, 128), HALF),
        )

    def piece_b(base, t, a, b):
        return (
            pl.ds(aligned(base + t * 128 + lax.div(a, 2) * 64 + b * 16, 16), 16),
            pl.ds(aligned(lax.rem(a, 2) * HALF, 128), HALF),
        )

    def around(ax, k):
        return lax.rem(at[ax] + k, 4)

    def some(span):
        return pl.ds(span[0], span[1])

    def gradient(g, left, right):
        send0[g] = dot_tn(left[:, far], right[...]).astype(bf16)
        send(send0.at[g], recv0.at[g], p_ss.at[g], p_rs.at[g], twin)
        sent.append((send0.at[g], p_ss.at[g]))
        part[g] = dot_tn(left[:, near], right[...])

    def step_a(span):
        gs, q = some(span), span[0]
        for g in range(span[0], span[0] + span[1]):
            take(recv0.at[g], p_rs.at[g])
            send_a[g] = (part[g] + recv0[g].astype(f32)).astype(bf16)
        for k in (2, 1, 3):
            for t in range(3):
                ax = axes[t][0]
                r, c = piece_a(0, t, around(ax, k))
                send(send_a.at[gs, r, c], recv_a.at[k - 1, t, gs], a_ss.at[q], a_rs.at[q], peer[ax](k))
        sent.append((recv_a.at[:, :, gs], a_ss.at[q]))

    def step_b(span):
        gs, q = some(span), span[0]
        take(recv_a.at[:, :, gs], a_rs.at[q])
        for t in range(3):
            ax = axes[t][1]
            r, c = piece_a(0, t, at[axes[t][0]])
            total = part[gs, r, c] + recv0[gs, r, c].astype(f32)
            for k in range(3):
                total = total + recv_a[k, t, gs].astype(f32)
            part_b[t, gs] = total
            send_b[t, gs] = total.astype(bf16)
            for k in (2, 1, 3):
                theirs = pl.ds(aligned(around(ax, k) * 16, 16), 16)
                send(send_b.at[t, gs, theirs], recv_b.at[k - 1, t, gs], b_ss.at[q], b_rs.at[q], peer[ax](k))
        sent.append((recv_b.at[:, :, gs], b_ss.at[q]))

    def step_c(span):
        gs, q = some(span), span[0]
        take(recv_b.at[:, :, gs], b_rs.at[q])
        for t in range(3):
            ax = axes[t][2]
            mine = pl.ds(aligned(at[axes[t][1]] * 16, 16), 16)
            total = part_b[t, gs, mine, :]
            for k in range(3):
                total = total + recv_b[k, t, gs].astype(f32)
            recv_c[pl.ds(at[ax], 1), t, gs] = total.astype(bf16)[None]
            block = recv_c.at[at[ax], t, gs]
            for k in (2, 1, 3):
                send(block, block, c_ss.at[q], c_rs.at[q], peer[ax](k))
        sent.append((recv_b.at[:, :, gs], c_ss.at[q]))

    def gather_b(span):
        gs, q = some(span), span[0]
        take(recv_b.at[:, :, gs], c_rs.at[q])
        for t in range(3):
            ax = axes[t][1]
            total = recv_c[0, t, gs].astype(f32)
            for k in (1, 2, 3):
                total = total + recv_c[k, t, gs].astype(f32)
            r, c = piece_b(core * HALF, t, at[axes[t][0]], at[ax])
            fin[gs, r, c] = total.astype(bf16)
            block = fin.at[gs, r, c]
            for k in (2, 1, 3):
                send(block, block, bg_ss.at[q], bg_rs.at[q], peer[ax](k))
        sent.append((recv_b.at[:, :, gs], bg_ss.at[q]))

    def to_twin(span, t, a):
        r, c = piece_a(core * HALF, t, a)
        block = fin.at[some(span), r, c]
        send(block, block, pg_ss.at[span[0]], pg_rs.at[span[0]], twin)

    def gather_a(span):
        gs, q = some(span), span[0]
        take(recv_b.at[:, :, gs], bg_rs.at[q])
        for k in (1, 3, 2):
            for t in range(3):
                ax = axes[t][0]
                r, c = piece_a(core * HALF, t, at[ax])
                block = fin.at[gs, r, c]
                send(block, block, ag_ss.at[q], ag_rs.at[q, k - 1], peer[ax](k))
        sent.append((recv_a.at[:, :, gs], ag_ss.at[q]))
        for t in range(3):
            to_twin(span, t, at[axes[t][0]])
        sent.append((fin.at[gs, near], pg_ss.at[q]))

    def gather_p(span, k):
        take(recv_a.at[k - 1, :, some(span)], ag_rs.at[span[0], k - 1])
        for t in range(3):
            to_twin(span, t, around(axes[t][0], 4 - k))

    def all_sent():
        for ref, sem in sent:
            take(ref, sem)
        sent.clear()

    def finish_near(span, *outs):
        for g, out in enumerate(outs, span[0]):
            out[near, :] = fin[g, near, :].astype(f32)

    def finish_far(span, *outs):
        take(fin.at[some(span), far], pg_rs.at[span[0]])
        for g, out in enumerate(outs, span[0]):
            out[far, :] = fin[g, far, :].astype(f32)

    def grad_mixed(i):
        rows = pl.ds(i * M, M)
        arrive("cot%d" % i)
        gmix[rows, :] = dot_nt(cot[rows, :], w_out[...]).astype(bf16)

    exchange(0, out1, got1, 0)
    arrive("w_out")
    grad_mixed(0)
    grad_mixed(1)
    out3[...] = dot(hot_t[R:K, :], gmix[...]).astype(bf16)
    exchange(1, out3, got3, 0)
    arrive("w_edge")
    means[0:R, :] = (dot(hot_t[0:R, :], msg[...]) * inv[0:R, 0:1]).astype(bf16)
    arrived(0, got1)
    counted = dot(tgt_t[...], got1[:, D:])
    inv[R:, :] = jnp.broadcast_to(
        1.0 / (counted[:, 0:1] + counted[:, S // 2 : S // 2 + 1] + 1.0), (H, S)
    )
    means[R:, :] = (dot(tgt_t[...], got1[:, 0:D]) * inv[R:, 0:1]).astype(bf16)
    hout[...] = dot(means[R:, :], w_edge[...]).astype(bf16)
    reply2[...] = dot_tn(tgt_t[...], hout[...]).astype(bf16)
    exchange(2, reply2, cat2, R)
    cat2[0:R, :] = dot(means[0:R, :], w_edge[...]).astype(bf16)
    hgrads[0:R, :] = dot(hot_t[0:R, :], gmix[...]).astype(bf16)
    arrived(1, got3)
    hgrads[R:, :] = dot(tgt_t[...], got3[...]).astype(bf16)
    gmean[...] = (dot_nt(hgrads[R:, :], w_edge[...]) * inv[R:, 0:1]).astype(bf16)
    reply4[...] = dot_tn(tgt_t[...], gmean[...]).astype(bf16)
    exchange(3, reply4, cat4, R)
    cat4[0:R, :] = (dot_nt(hgrads[0:R, :], w_edge[...]) * inv[0:R, 0:1]).astype(bf16)
    gradient(WEDGE, means, hgrads)
    arrived(2, cat2)
    for i in range(N // M):
        rows = pl.ds(i * M, M)
        mixed[rows, :] = dot_tn(hot_t[:, rows], cat2[...]).astype(bf16)
    gradient(WOUT, mixed, cot)
    arrived(3, cat4)
    for i in range(N // M):
        rows = pl.ds(i * M, M)
        gpre[rows, :] = (dot_tn(hot_t[:, rows], cat4[...]) * dact[rows, :].astype(f32)).astype(bf16)
    step_a(BOTH)
    gradient(WIN, cells, gpre)
    step_a(LAST)

    def layer_out(i):
        rows = pl.ds(i * M, M)
        mixed[rows, :] = (cells[rows, :].astype(f32) + dot(mixed[rows, :], w_out[...])).astype(bf16)

    def grad_cells(start, n):
        rows = pl.ds(start, n)
        gpre[rows, :] = (cot[rows, :].astype(f32) + dot_nt(gpre[rows, :], w_in[...])).astype(bf16)

    layer_out(0)
    step_b(BOTH)
    layer_out(1)
    step_b(LAST)
    grad_cells(0, M)
    step_c(BOTH)
    grad_cells(M, M // 2)
    step_c(LAST)
    grad_cells(M + M // 2, M // 2)
    all_sent()
    gather_b(BOTH)
    gather_b(LAST)
    gather_a(BOTH)
    gather_a(LAST)
    for span in (BOTH, LAST):
        for k in (1, 3, 2):
            gather_p(span, k)
    finish_near(BOTH, wedge_ref, wout_ref)
    finish_near(LAST, win_ref)
    finish_far(BOTH, wedge_ref, wout_ref)
    finish_far(LAST, win_ref)
    all_sent()


def write(*refs):
    n = len(refs) // 2
    copies = [
        pltpu.make_async_copy(refs[i], refs[n + i], refs[2 * n].at[i]) for i in range(n)
    ]
    for copy in copies:
        copy.start()
    for copy in copies:
        copy.wait()


def per_device(cells_in, w_in, w_edge, w_out, cotangent, cell_row, send_slot, recv_target):
    any_spec = pl.BlockSpec(memory_space=pl.ANY)
    vmem = pl.BlockSpec(memory_space=pltpu.VMEM)
    dma = pltpu.SemaphoreType.DMA
    scratch = [
        pltpu.VMEM((1, N), jnp.int32),
        pltpu.VMEM((2, N), jnp.int32),
        pltpu.VMEM((1, S), jnp.int32),
        pltpu.VMEM((N, D), bf16),
        pltpu.VMEM((N, D), bf16),
        pltpu.VMEM((D, D), bf16),
        pltpu.VMEM((D, D), bf16),
        pltpu.VMEM((D, D), bf16),
        pltpu.VMEM((N, D), bf16),
        pltpu.VMEM((K, N), bf16),
        pltpu.VMEM((R + H, D), bf16),
        pltpu.VMEM((R + H, D), bf16),
        pltpu.VMEM((H, D), bf16),
        pltpu.VMEM((H, D), bf16),
        pltpu.VMEM((H, S), bf16),
        pltpu.VMEM((R + H, S), f32),
        pltpu.VMEM((S, D + S), bf16),
        pltpu.VMEM((S, D), bf16),
        pltpu.VMEM((S, D + S), bf16),
        pltpu.VMEM((S, D), bf16),
        pltpu.VMEM((S, D), bf16),
        pltpu.VMEM((S, D), bf16),
        pltpu.VMEM((K, D), bf16),
        pltpu.VMEM((K, D), bf16),
        pltpu.VMEM((3, HALF, D), bf16),
        pltpu.VMEM((3, HALF, D), bf16),
        pltpu.VMEM((3, HALF, D), f32),
        pltpu.VMEM((3, HALF, D), bf16),
        pltpu.VMEM((3, 3, 3, 64, HALF), bf16),
        pltpu.VMEM((3, 3, 64, HALF), f32),
        pltpu.VMEM((3, 3, 64, HALF), bf16),
        pltpu.VMEM((3, 3, 3, 16, HALF), bf16),
        pltpu.VMEM((4, 3, 3, 16, HALF), bf16),
        pltpu.VMEM((3, D, D), bf16),
        dma((10,)),
        dma((4,)),
        dma((4,)),
        dma((3,)),
        dma((3,)),
        dma((3,)),
        dma((3,)),
        dma((3,)),
        dma((3,)),
        dma((3,)),
        dma((3,)),
        dma((3,)),
        dma((3,)),
        dma((3,)),
        dma((3, 3)),
        dma((3,)),
        dma((3,)),
    ]
    results = pl.pallas_call(
        kernel,
        out_shape=(
            pltpu.VMEM((N, D), bf16),
            pltpu.VMEM((N, D), bf16),
            pltpu.VMEM((D, D), f32),
            pltpu.VMEM((D, D), f32),
            pltpu.VMEM((D, D), f32),
        ),
        in_specs=[any_spec] * 8,
        out_specs=[vmem] * 5,
        scratch_shapes=scratch,
        compiler_params=pltpu.CompilerParams(
            collective_id=0, has_side_effects=True, vmem_limit_bytes=44 * 2**20
        ),
        name="layer",
    )(
        cells_in, w_in, w_edge, w_out, cotangent,
        cell_row.reshape(1, N), send_slot, recv_target,
    )
    outs = tuple(jax.ShapeDtypeStruct(r.shape, r.dtype) for r in results)
    return pl.pallas_call(
        write,
        out_shape=outs,
        in_specs=[any_spec] * 5,
        out_specs=[any_spec] * 5,
        scratch_shapes=[dma((5,))],
        compiler_params=pltpu.CompilerParams(vmem_limit_bytes=2**20),
        name="write",
    )(*results)


def solution(mesh):
    placed = (
        P(("cells", "edges"), None),
        P(),
        P(),
        P(),
        P(("cells", "edges"), None),
        P(("cells", "edges")),
        P(None, ("cells", "edges")),
        P(("cells", "edges"), None),
    )
    return jax.shard_map(
        per_device,
        mesh=mesh,
        in_specs=placed,
        out_specs=(P(("cells", "edges"), None), P(("cells", "edges"), None), P(), P(), P()),
        check_vma=False,
    )
```
